256 devices in a mesh: section: 8 (over x, core), dp: 16 (over y_hi, z), mp: 2 (over y_lo).
Axes of the slice: x: 4, y: 4 (y_hi: 2, y_lo: 2; y = y_hi * 2 + y_lo), z: 8, core: 2. Of those that a mesh axis runs over, the one named last changes fastest.
Arguments:
- nbr_states: bfloat16 [4096, 8192], P('dp'), may hold values from -6 to 6
- kv_weight: bfloat16 [8192, 2, 4096], P(None, None, ('section', 'mp')), may hold values from -0.0625 to 0.0625
- queries: bfloat16 [4096, 4096], P('dp', ('section', 'mp')), may hold values from -36 to 36
- out_grad: bfloat16 [4096, 4096], P('dp', ('section', 'mp')), may hold values from -6 to 6
- citations: int32 [64, 2], P('dp'), may hold values from 0 to 31, as said below
Outputs:
- attended: bfloat16 [4096, 4096], P('dp', ('section', 'mp'))
- nbr_grad: bfloat16 [4096, 8192], P('dp', ('section', 'mp'))
The draws below stay inside these ranges and needn't reach their ends.
Inputs may be any that keep to these rules, and one draw needn't show every extreme that they name: `citations`: owner of id i is i // 2. The two ids of one decoder block have different owners; all ids that the 4 blocks of one dp index cite from one owner are equal.
All inputs are finite; a program needn't handle non-finite values.
Results may differ from the reference program's by a relative error of at most 0.012.
The reference program's roundings to bfloat16 on the way count: a program that leaves them out, or rounds other values in their place, can miss the bound.
Values may be sent and summed in bfloat16 or wider, within the bound.
A program may use at most 128 MiB of HBM per device.

```python
import jax
import jax.numpy as jnp
from jax import lax

D = 8192
HEADS = 32
HS = 128
CH = 64
CL = 128
NCH_DEV = 2
DCH_DEV = 4
NROWS = 4096
DROWS = 4096
N_DP = 16


def draw_queries(key, part):
    key = jax.random.fold_in(key, 5)
    values = jnp.clip(jax.random.normal(key, (DROWS, HEADS * HS), jnp.float32), -6.0, 6.0)
    return values.astype(jnp.bfloat16)


def draw_citations(key, part):
    key = jax.random.fold_in(key, 11)
    keys = jax.random.split(key, 5)
    count = DCH_DEV * N_DP
    ranking = jax.random.permutation(keys[0], N_DP)
    first_pick = jax.random.randint(keys[1], (count,), 0, N_DP)
    second_pick = jax.random.randint(keys[2], (count,), 0, N_DP)
    first = ranking[jnp.minimum(first_pick, second_pick)]
    offset = jax.random.randint(keys[3], (count,), 1, N_DP)
    second = (first + offset) % N_DP
    table = jax.random.randint(keys[4], (N_DP, N_DP), 0, NCH_DEV)
    device = jnp.arange(count) // DCH_DEV
    owners = jnp.stack([first, second], axis=1)
    within = table[device[:, None], owners]
    return (owners * NCH_DEV + within).astype(jnp.int32)


def block_scale(own_key, dims, cuts, least, largest):
    factor_of, own = 1.0, jax.random.fold_in(own_key, 6)
    for dim, shards_of in cuts:
        steps = jnp.exp(jax.random.uniform(jax.random.fold_in(own, dim), (shards_of,), jnp.float32, least / len(cuts), largest / len(cuts)))
        factor_of = factor_of * jnp.repeat(steps, dims[dim] // shards_of).reshape([-1 if axis == dim else 1 for axis in range(len(dims))])
    return factor_of


def bell_draw(own_key, dims, spread, most, pieces=(), dtype=jnp.bfloat16):
    loudness = block_scale(own_key, dims, pieces, -0.22, 0.18) if pieces else 1.0
    values = jax.random.normal(own_key, dims, jnp.float32) * spread * loudness
    return jnp.minimum(jnp.maximum(values, -most), most).astype(dtype)


def setup_inputs(seed: int = 0) -> dict:
    splits = jax.random.split(jax.random.key(seed), 6)
    return {
        "nbr_states": bell_draw(splits[0], (NROWS, D), 1.0, 6.0, ((0, 16),)),
        "kv_weight": bell_draw(splits[1], (D, 2, HEADS * HS), D ** -0.5, 0.0625, ((2, 16),)),
        "queries": draw_queries(jax.random.fold_in(splits[5], 71), 0),
        "out_grad": bell_draw(splits[3], (DROWS, HEADS * HS), 1.0, 6.0, ((0, 16), (1, 16))),
        "citations": draw_citations(jax.random.fold_in(splits[5], 71), 0),
    }


def reference(nbr_states, kv_weight, queries, out_grad, citations):
    hidden = HEADS * HS
    flat_weight = kv_weight.reshape(D, 2 * hidden)
    enc_rows = jnp.dot(nbr_states, flat_weight, preferred_element_type=jnp.float32).astype(jnp.bfloat16)
    enc_rows = enc_rows.reshape(NCH_DEV * N_DP, CL, 2, HEADS, HS)
    query_all = queries.reshape(-1, CH, HEADS, HS)
    cotangent = out_grad.reshape(-1, CH, HEADS, HS)
    scaling = 1.0 / (HS ** 0.5)

    def one_block(carry, item):
        query_rows, out_rows, block_ids = item
        neighbours = enc_rows[block_ids]
        key_rows = neighbours[:, :, 0].reshape(2 * CL, HEADS, HS).astype(jnp.float32)
        value_rows = neighbours[:, :, 1].reshape(2 * CL, HEADS, HS).astype(jnp.float32)
        query_f = query_rows.astype(jnp.float32)
        out_f = out_rows.astype(jnp.float32)
        scores = jnp.einsum('qhd,khd->hqk', query_f, key_rows) * scaling
        attn_prob = jax.nn.softmax(scores, axis=-1)
        rounded = lax.optimization_barrier(attn_prob.astype(jnp.bfloat16)).astype(jnp.float32)
        attended = jnp.einsum('hqk,khd->qhd', rounded, value_rows).astype(jnp.bfloat16)
        value_grad = jnp.einsum('hqk,qhd->khd', rounded, out_f)
        prob_grad = jnp.einsum('qhd,khd->hqk', out_f, value_rows)
        score_grad = attn_prob * (prob_grad - jnp.sum(prob_grad * attn_prob, axis=-1, keepdims=True))
        score_grad = lax.optimization_barrier(score_grad.astype(jnp.bfloat16)).astype(jnp.float32)
        key_grad = jnp.einsum('hqk,qhd->khd', score_grad, query_f) * scaling
        row_grads = jnp.stack([key_grad.reshape(2, CL, HEADS, HS), value_grad.reshape(2, CL, HEADS, HS)], axis=2)
        carry = carry.at[block_ids].add(row_grads)
        return carry, attended

    start = jnp.zeros((NCH_DEV * N_DP, CL, 2, HEADS, HS), jnp.float32)
    kv_grad, outputs = lax.scan(one_block, start, (query_all, cotangent, citations))
    attended = outputs.reshape(-1, hidden)
    flat_grad = kv_grad.astype(jnp.bfloat16).reshape(NCH_DEV * N_DP * CL, 2 * hidden)
    nbr_grad = lax.dot_general(flat_grad, flat_weight, (((1,), (1,)), ((), ())), preferred_element_type=jnp.float32)
    return attended, nbr_grad.astype(jnp.bfloat16)
```

```python
import functools

import jax
import jax.numpy as jnp
from jax import lax
from jax.experimental import pallas as pl
from jax.experimental.pallas import tpu as pltpu
from jax.sharding import PartitionSpec as P

HS = 128
CH = 64
CL = 128
NZ = 8
NX = 4
KC = 8
NEG = -1e30
BF = jnp.bfloat16
F32 = jnp.float32
NT = (((1,), (1,)), ((), ()))
NN = (((1,), (0,)), ((), ()))
TN = (((0,), (0,)), ((), ()))


def dot(a, b, dims):
    return lax.dot_general(a, b, dims, preferred_element_type=F32)


def kernel(
    cit_ref, q_ref, g_ref, x_hbm, w_hbm, att_ref, nbr_ref,
    X, W, acc, G, KV, info_out, info_in, E, DP, st_out, st_in, res_out, res_in,
    at_out, at_in, GR, yg_out, yg_in, kvg, cs_out, cs_in, R, by_in, RB,
    ax_in, ax_tmp, bx_in, bx_tmp, ay_out, ay_in,
    ld_sem, ag_send, ag_recv, kv_send, kv_recv, inf_send, inf_recv, st_send, st_recv,
    rs_send, rs_recv, at_send, at_recv, yg_send, yg_recv, cs_send, cs_recv,
    by_send, by_recv, ax_send, ax_recv, bx_send, bx_recv, ay_send, ay_recv,
):
    s, d, m = lax.axis_index("section"), lax.axis_index("dp"), lax.axis_index("mp")
    x, c = s // 2, s % 2
    yh, z = d // NZ, d % NZ
    depth = x_hbm.shape[1] // KC
    scaling = 1.0 / HS**0.5

    def at_z(zt):
        return {"dp": yh * NZ + zt}

    y_mate = {"dp": (1 - yh) * NZ + z}
    core_mate = {"section": x * 2 + (1 - c)}
    x_right = {"section": lax.rem(x + 1, NX) * 2 + c}
    x_left = {"section": lax.rem(x + NX - 1, NX) * 2 + c}
    m_mate = {"mp": 1 - m}

    def remote(src, dst, ssem, rsem, dev):
        return pltpu.make_async_remote_copy(
            src_ref=src, dst_ref=dst, send_sem=ssem, recv_sem=rsem,
            device_id=dev, device_id_type=pl.DeviceIdType.MESH,
        )

    def x_load(k):
        return pltpu.make_async_copy(
            x_hbm.at[:, pl.ds(pl.multiple_of(k * depth, depth), depth)], X.at[k], ld_sem.at[2, k]
        )

    def w_load(h, k):
        rows = pl.ds(pl.multiple_of(k * depth, depth), depth)
        return pltpu.make_async_copy(
            w_hbm.at[rows, pl.ds(h * 256, 256)], W.at[rows, pl.ds(h * 256, 256)], ld_sem.at[h, k]
        )

    def start_loads(k, _):
        x_load(k).start()
        w_load(0, k).start()
        return 0

    lax.fori_loop(0, KC, start_loads, 0)

    def start_loads_1(k, _):
        w_load(1, k).start()
        return 0

    lax.fori_loop(0, KC, start_loads_1, 0)

    barrier = pltpu.get_barrier_semaphore()
    for dev in [at_z(lax.rem(z + r, NZ)) for r in range(1, NZ)] + [
        y_mate, core_mate, x_right, x_left, m_mate
    ]:
        pl.semaphore_signal(barrier, inc=1, device_id=dev, device_id_type=pl.DeviceIdType.MESH)

    G[z, 0] = q_ref[...]
    G[z, 1] = g_ref[...]
    lane = lax.broadcasted_iota(jnp.int32, (16, 256), 1) // CH
    owner = lax.broadcasted_iota(jnp.int32, (16, 256), 0)
    ids = []
    for k in range(2):
        v = jnp.zeros((16, 256), jnp.int32)
        for b in range(4):
            v = jnp.where(lane == b, cit_ref[b, k], v)
        ids.append(v)
    second = (ids[0] == owner * 2 + 1) | (ids[1] == owner * 2 + 1)
    first = (ids[0] == owner * 2) | (ids[1] == owner * 2)
    cited = jnp.where(first | second, 1.0, 0.0).astype(F32)
    sel = jnp.where(second, 1.0, 0.0).astype(F32)
    sel = jnp.max(sel, axis=1, keepdims=True) + jnp.zeros((16, 256), F32)
    for t in range(NZ):
        for w in range(2):
            o = w * NZ + t
            info_out[t, w : w + 1, :] = cited[o : o + 1]
            info_out[t, 2 + w : 3 + w, :] = sel[o : o + 1]
        info_out[t, 4:8, :] = jnp.zeros((4, 256), F32)
    info_in[z] = info_out[z]
    pl.semaphore_wait(barrier, 12)

    def ag(direction, arr, t):
        if direction == 0:
            home, to = lax.rem(z - t + NZ, NZ), lax.rem(z + 1, NZ)
        else:
            home, to = lax.rem(z + t, NZ), lax.rem(z + NZ - 1, NZ)
        return remote(
            G.at[home, arr], G.at[home, arr],
            ag_send.at[direction, arr, t], ag_recv.at[direction, arr, t], at_z(to),
        )

    for direction in range(2):
        for arr in range(2):
            ag(direction, arr, 0).start()

    def info_copy(r):
        to = lax.rem(z + r, NZ)
        return remote(info_out.at[to], info_in.at[z], inf_send.at[r], inf_recv.at[r], at_z(to))

    def info_start(r, _):
        info_copy(r).start()
        return 0

    lax.fori_loop(1, NZ, info_start, 0)

    def kv_copy(h):
        return remote(KV.at[yh, h], KV.at[yh, h], kv_send.at[h], kv_recv.at[h], y_mate)

    for h in range(2):
        acc[...] = jnp.zeros_like(acc)

        def piece(k, _):
            if h == 0:
                x_load(k).wait()
            w_load(h, k).wait()
            rows = pl.ds(pl.multiple_of(k * depth, depth), depth)
            acc[...] += dot(X[k], W[rows, h * 256 : h * 256 + 256], NN)
            return 0

        lax.fori_loop(0, KC, piece, 0)
        KV[yh, h] = acc[...].astype(BF)
        kv_copy(h).start()

    def kv_wait(h):
        pltpu.make_async_remote_copy(
            src_ref=KV.at[1 - yh, h], dst_ref=KV.at[1 - yh, h], send_sem=kv_send.at[h],
            recv_sem=kv_recv.at[h], device_id=y_mate, device_id_type=pl.DeviceIdType.MESH,
        ).wait_recv()

    def info_wait(r, _):
        info_copy(r).wait_recv()
        return 0

    lax.fori_loop(1, NZ, info_wait, 0)
    for h in range(2):
        kv_wait(h)

    def chosen(j, h):
        out = []
        for w in range(2):
            f = info_in[j, 2 + w : 3 + w, :] + jnp.zeros((CL, 256), F32)
            one, zero = f.astype(BF), (1.0 - f).astype(BF)
            out.append(KV[w, h, 0:CL, :] * zero + KV[w, h, CL : 2 * CL, :] * one)
        return jnp.concatenate(out, axis=0)

    def st_copy(j):
        r = lax.rem(j - z + NZ, NZ)
        return remote(st_out.at[j], st_in.at[z], st_send.at[r], st_recv.at[r], at_z(j))

    def att1(j):
        for h in range(2):
            kv = chosen(j, h)
            cols = slice(h * HS, h * HS + HS)
            sc = dot(kv[:, :HS], G[j, 0, :, cols], NT) * scaling
            sc = jnp.concatenate(
                [
                    jnp.where(info_in[j, w : w + 1, :] > 0.0, sc[w * CL : w * CL + CL], NEG)
                    for w in range(2)
                ],
                axis=0,
            )
            top = jnp.max(sc, axis=0, keepdims=True)
            e = jnp.exp(sc - top)
            dp = dot(kv[:, HS:], G[j, 1, :, cols], NT)
            E[j, h] = e
            DP[j, h] = dp
            st_out[j, 3 * h : 3 * h + 1, :] = top
            st_out[j, 3 * h + 1 : 3 * h + 2, :] = jnp.sum(e, axis=0, keepdims=True)
            st_out[j, 3 * h + 2 : 3 * h + 3, :] = jnp.sum(e * dp, axis=0, keepdims=True)
        st_out[j, 6:8, :] = jnp.zeros((2, 256), F32)

    def hop(t, _):
        @pl.when(t > 0)
        def _():
            ag(0, 0, t - 1).wait_recv()
            ag(1, 1, t - 1).wait_recv()

            @pl.when(t < 4)
            def _():
                ag(0, 0, t).start()
                ag(1, 1, t).start()
                ag(0, 1, t - 1).wait_recv()
                ag(1, 0, t - 1).wait_recv()

                @pl.when(t < 3)
                def _():
                    ag(0, 1, t).start()
                    ag(1, 0, t).start()

        def side(i, _):
            j = lax.rem(z + NZ - t + 2 * i * t, NZ)
            att1(j)

            @pl.when(t > 0)
            def _():
                st_copy(j).start()

            return 0

        lax.fori_loop(0, jnp.where((t == 0) | (t == 4), 1, 2), side, 0)
        return 0

    lax.fori_loop(0, 5, hop, 0)

    st_in[z] = st_out[z]

    def st_wait(r, _):
        src = lax.rem(z + NZ - r, NZ)
        remote(st_out.at[src], st_in.at[src], st_send.at[r], st_recv.at[r], at_z(src)).wait_recv()
        return 0

    lax.fori_loop(1, NZ, st_wait, 0)
    for h in range(2):
        tops = [st_in[i, 3 * h : 3 * h + 1, :] for i in range(NZ)]
        top = functools.reduce(jnp.maximum, tops)
        total = jnp.zeros((1, 256), F32)
        dots = jnp.zeros((1, 256), F32)
        for i in range(NZ):
            f = jnp.exp(tops[i] - top)
            total += f * st_in[i, 3 * h + 1 : 3 * h + 2, :]
            dots += f * st_in[i, 3 * h + 2 : 3 * h + 3, :]
        res_out[3 * h : 3 * h + 1, :] = top
        res_out[3 * h + 1 : 3 * h + 2, :] = 1.0 / total
        res_out[3 * h + 2 : 3 * h + 3, :] = dots / total
    res_out[6:8, :] = jnp.zeros((2, 256), F32)
    res_in[z] = res_out[...]

    def res_copy(r):
        return remote(res_out, res_in.at[z], rs_send.at[r], rs_recv.at[r], at_z(lax.rem(z + r, NZ)))

    def res_start(r, _):
        res_copy(r).start()
        return 0

    lax.fori_loop(1, NZ, res_start, 0)
    GR[...] = jnp.zeros_like(GR)

    def at_copy(j):
        r = lax.rem(j - z + NZ, NZ)
        return remote(at_out.at[j], at_in.at[z], at_send.at[r], at_recv.at[r], at_z(j))

    def att2(r, _):
        j = lax.rem(z + NZ - r, NZ)

        @pl.when(r > 0)
        def _():
            remote(res_out, res_in.at[j], rs_send.at[r], rs_recv.at[r], at_z(j)).wait_recv()

        for h in range(2):
            cols = slice(h * HS, h * HS + HS)
            f = jnp.exp(st_out[j, 3 * h : 3 * h + 1, :] - res_in[j, 3 * h : 3 * h + 1, :])
            p = E[j, h] * (f * res_in[j, 3 * h + 1 : 3 * h + 2, :])
            rounded = p.astype(BF)
            ds = (p * (DP[j, h] - res_in[j, 3 * h + 2 : 3 * h + 3, :])).astype(BF)
            kg = dot(ds, G[j, 0, :, cols], NN) * scaling
            vg = dot(rounded, G[j, 1, :, cols], NN)
            part = jnp.concatenate([kg, vg], axis=1)
            for w in range(2):
                one = info_in[j, 2 + w : 3 + w, :]
                mine = part[w * CL : w * CL + CL]
                GR[w, 0:CL, h * 256 : h * 256 + 256] += mine * (1.0 - one)
                GR[w, CL : 2 * CL, h * 256 : h * 256 + 256] += mine * one
            values = chosen(j, h)[:, HS:]
            at_out[j, cols, :] = dot(values, rounded, TN).astype(BF)

        @pl.when(r > 0)
        def _():
            at_copy(j).start()

        return 0

    lax.fori_loop(0, NZ, att2, 0)
    at_in[z] = at_out[z]

    yg_out[...] = GR[1 - yh].astype(BF)
    yg = remote(yg_out, yg_in, yg_send, yg_recv, y_mate)
    yg.start()
    yg.wait_recv()
    kvg[...] = (GR[yh] + yg_in[...].astype(F32)).astype(BF)

    def w_rows(i, core):
        e = ((i // 2) * 2 + core) * 2 + i % 2
        return W[pl.ds(pl.multiple_of(e * 512, 512), 512), :]

    def cs_copy(i):
        return remote(cs_out.at[i], cs_in.at[i], cs_send.at[i], cs_recv.at[i], core_mate)

    def to_core(i, _):
        cs_out[i] = dot(kvg[...], w_rows(i, 1 - c), NT).astype(BF)
        cs_copy(i).start()
        return 0

    lax.fori_loop(0, 8, to_core, 0)

    def own_core(i, _):
        own = dot(kvg[...], w_rows(i, c), NT)
        cs_copy(i).wait_recv()
        R[i // 2, i % 2] = (own + cs_in[i].astype(F32)).astype(BF)
        return 0

    lax.fori_loop(0, 8, own_core, 0)

    two, nxt, prv = lax.rem(x + 2, NX), lax.rem(x + 1, NX), lax.rem(x + 3, NX)

    def xsum(src, tmp, into, ssem, rsem):
        def at(i, half):
            return src(i, slice(half * 256, half * 256 + 256))

        firsts = [
            remote(at(two, 0), into.at[0], ssem.at[0], rsem.at[0], x_right),
            remote(at(two, 1), into.at[1], ssem.at[1], rsem.at[1], x_left),
            remote(at(nxt, 1), into.at[2], ssem.at[2], rsem.at[2], x_right),
            remote(at(prv, 0), into.at[3], ssem.at[3], rsem.at[3], x_left),
        ]
        seconds = [
            remote(tmp.at[0], into.at[4], ssem.at[4], rsem.at[4], x_right),
            remote(tmp.at[1], into.at[5], ssem.at[5], rsem.at[5], x_left),
        ]

        def relay():
            for i, (to, half) in enumerate([(nxt, 0), (prv, 1)]):
                firsts[i].wait_recv()
                tmp[i] = (at(to, half)[...].astype(F32) + into[i].astype(F32)).astype(BF)
                seconds[i].start()

        def finish():
            firsts[2].wait_recv()
            firsts[3].wait_recv()
            seconds[0].wait_recv()
            seconds[1].wait_recv()
            halves = []
            for half, got in [(0, (4, 3)), (1, (2, 5))]:
                v = at(x, half)[...].astype(F32)
                for g in got:
                    v += into[g].astype(F32)
                halves.append(v)
            return halves

        def start():
            for cp in firsts:
                cp.start()

        def drain():
            for cp in firsts + seconds:
                cp.wait_send()

        return start, relay, finish, drain

    a_start, a_relay, a_finish, a_drain = xsum(
        lambda i, cols: R.at[i, :, 0:CL, cols], ax_tmp, ax_in, ax_send, ax_recv
    )
    b_start, b_relay, b_finish, b_drain = xsum(
        lambda i, cols: RB.at[i, :, cols], bx_tmp, bx_in, bx_send, bx_recv
    )
    by = remote(R.at[:, 1 - m, CL : 2 * CL, :], by_in, by_send, by_recv, m_mate)
    a_start()
    by.start()
    a_relay()
    by.wait_recv()

    def add_b(i, _):
        RB[i] = (R[i, m, CL : 2 * CL, :].astype(F32) + by_in[i].astype(F32)).astype(BF)
        return 0

    lax.fori_loop(0, NX, add_b, 0)
    b_start()
    fa = a_finish()
    for half in range(2):
        cols = slice(half * 256, half * 256 + 256)
        ay_out[:, :, cols] = fa[half].astype(BF)
    ay = remote(ay_out.at[1 - m], ay_in, ay_send, ay_recv, m_mate)
    ay.start()
    b_relay()

    def at_wait(r, _):
        src = lax.rem(z + NZ - r, NZ)
        remote(at_out.at[src], at_in.at[src], at_send.at[r], at_recv.at[r], at_z(src)).wait_recv()
        return 0

    lax.fori_loop(1, NZ, at_wait, 0)
    total = at_in[0].astype(F32)
    for i in range(1, NZ):
        total += at_in[i].astype(F32)
    att_ref[...] = total.T.astype(BF)

    fb = b_finish()
    for half in range(2):
        cols = slice(half * 256, half * 256 + 256)
        nbr_ref[CL : 2 * CL, cols] = fb[half].astype(BF)
    ay.wait_recv()
    nbr_ref[0:CL, :] = (ay_out[m].astype(F32) + ay_in[...].astype(F32)).astype(BF)

    for direction in range(2):
        for arr in range(2):
            for t in range(4 if direction == arr else 3):
                ag(direction, arr, t).wait_send()
    for h in range(2):
        kv_copy(h).wait_send()

    def sent(r, _):
        j = lax.rem(z + r, NZ)
        info_copy(r).wait_send()
        st_copy(j).wait_send()
        res_copy(r).wait_send()
        at_copy(j).wait_send()
        return 0

    lax.fori_loop(1, NZ, sent, 0)
    yg.wait_send()

    def cs_sent(i, _):
        cs_copy(i).wait_send()
        return 0

    lax.fori_loop(0, 8, cs_sent, 0)
    by.wait_send()
    ay.wait_send()
    a_drain()
    b_drain()


def on_device(nbr_states, kv_weight, queries, out_grad, citations):
    width = kv_weight.shape[0]
    weight = kv_weight.reshape(width, 2, 2, HS).transpose(0, 2, 1, 3).reshape(width, 4 * HS)
    V, D = pltpu.VMEM, pltpu.SemaphoreType.DMA
    scratch = [
        V((KC, 256, width // KC), BF),
        V((width, 512), BF),
        V((256, 256), F32),
        V((NZ, 2, 256, 256), BF),
        V((2, 2, 256, 256), BF),
        V((NZ, 8, 256), F32),
        V((NZ, 8, 256), F32),
        V((NZ, 2, 256, 256), F32),
        V((NZ, 2, 256, 256), F32),
        V((NZ, 8, 256), F32),
        V((NZ, 8, 256), F32),
        V((8, 256), F32),
        V((NZ, 8, 256), F32),
        V((NZ, 256, 256), BF),
        V((NZ, 256, 256), BF),
        V((2, 256, 512), F32),
        V((256, 512), BF),
        V((256, 512), BF),
        V((256, 512), BF),
        V((8, 256, 512), BF),
        V((8, 256, 512), BF),
        V((NX, 2, 256, 512), BF),
        V((NX, CL, 512), BF),
        V((NX, CL, 512), BF),
        V((6, 2, CL, 256), BF),
        V((2, 2, CL, 256), BF),
        V((6, CL, 256), BF),
        V((2, CL, 256), BF),
        V((2, CL, 512), BF),
        V((CL, 512), BF),
        D((3, KC)),
        D((2, 2, 4)), D((2, 2, 4)),
        D((2,)), D((2,)),
        D((NZ,)), D((NZ,)),
        D((NZ,)), D((NZ,)),
        D((NZ,)), D((NZ,)),
        D((NZ,)), D((NZ,)),
        D, D,
        D((8,)), D((8,)),
        D, D,
        D((6,)), D((6,)),
        D((6,)), D((6,)),
        D, D,
    ]
    vmem = pl.BlockSpec(memory_space=pltpu.VMEM)
    hbm = pl.BlockSpec(memory_space=pl.ANY)
    return pl.pallas_call(
        kernel,
        out_shape=(
            jax.ShapeDtypeStruct((256, 256), BF),
            jax.ShapeDtypeStruct((256, 512), BF),
        ),
        in_specs=[pl.BlockSpec(memory_space=pltpu.SMEM), vmem, vmem, hbm, hbm],
        out_specs=(vmem, vmem),
        scratch_shapes=scratch,
        compiler_params=pltpu.CompilerParams(
            collective_id=0, has_side_effects=True, vmem_limit_bytes=56 * 2**20
        ),
        cost_estimate=pl.CostEstimate(
            flops=6 * 10**9, bytes_accessed=13 * 2**20, transcendentals=2 * 10**6
        ),
    )(citations, queries, out_grad, nbr_states, weight)


def solution(mesh):
    heads = ("section", "mp")
    return jax.shard_map(
        on_device,
        mesh=mesh,
        in_specs=(
            P("dp", None),
            P(None, None, heads),
            P("dp", heads),
            P("dp", heads),
            P("dp", None),
        ),
        out_specs=(P("dp", heads), P("dp", heads)),
        check_vma=False,
    )
```

```python
import functools

import jax
import jax.numpy as jnp
from jax import lax
from jax.experimental import pallas as pl
from jax.experimental.pallas import tpu as pltpu
from jax.sharding import PartitionSpec as P

HS = 128
CH = 64
CL = 128
NZ = 8
NX = 4
KC = 8
ROWS_A = 144
NEG = -1e30
BF = jnp.bfloat16
F32 = jnp.float32
NT = (((1,), (1,)), ((), ()))
NN = (((1,), (0,)), ((), ()))
TN = (((0,), (0,)), ((), ()))


def dot(a, b, dims):
    return lax.dot_general(a, b, dims, preferred_element_type=F32)


def kernel(
    cit_ref, q_ref, g_ref, x_hbm, w_hbm, att_ref, nbr_ref,
    X, W32, W, acc, G, KV, info_out, info_in, E, DP, st_out, st_in, res_out, res_in,
    at_out, at_in, GR, yg_out, yg_in, kvg, cs_out, cs_in, R, by_in, RB,
    ax_in, ax_tmp, bx_in, bx_tmp, ay_out, ay_in, PM,
    ld_sem, ag_send, ag_recv, kv_send, kv_recv, inf_send, inf_recv, st_send, st_recv,
    rs_send, rs_recv, at_send, at_recv, yg_send, yg_recv, cs_send, cs_recv,
    by_send, by_recv, ax_send, ax_recv, bx_send, bx_recv, ay_send, ay_recv,
):
    s, d, m = lax.axis_index("section"), lax.axis_index("dp"), lax.axis_index("mp")
    x, c = s // 2, s % 2
    yh, z = d // NZ, d % NZ
    depth = x_hbm.shape[1] // KC
    scaling = 1.0 / HS**0.5

    def at_z(zt):
        return {"dp": yh * NZ + zt}

    y_mate = {"dp": (1 - yh) * NZ + z}
    core_mate = {"section": x * 2 + (1 - c)}
    x_right = {"section": lax.rem(x + 1, NX) * 2 + c}
    x_left = {"section": lax.rem(x + NX - 1, NX) * 2 + c}
    m_mate = {"mp": 1 - m}

    def remote(src, dst, ssem, rsem, dev):
        return pltpu.make_async_remote_copy(
            src_ref=src, dst_ref=dst, send_sem=ssem, recv_sem=rsem,
            device_id=dev, device_id_type=pl.DeviceIdType.MESH,
        )

    def x_load(k):
        return pltpu.make_async_copy(
            x_hbm.at[:, pl.ds(pl.multiple_of(k * depth, depth), depth)], X.at[k], ld_sem.at[1, k]
        )

    def w_load(k):
        return pltpu.make_async_copy(
            w_hbm.at[pl.ds(pl.multiple_of(k * 4 * depth, depth), 4 * depth), :], W32.at[k], ld_sem.at[0, k]
        )

    def start_loads(k, _):
        w_load(k).start()
        x_load(k).start()
        return 0

    lax.fori_loop(0, KC, start_loads, 0)

    barrier = pltpu.get_barrier_semaphore()
    for dev in [at_z(lax.rem(z + r, NZ)) for r in range(1, NZ)] + [
        y_mate, core_mate, x_right, x_left, m_mate
    ]:
        pl.semaphore_signal(barrier, inc=1, device_id=dev, device_id_type=pl.DeviceIdType.MESH)

    G[z, 0] = q_ref[...]
    G[z, 1] = g_ref[...]
    lane = lax.broadcasted_iota(jnp.int32, (16, 256), 1) // CH
    owner = lax.broadcasted_iota(jnp.int32, (16, 256), 0)
    ids = []
    for k in range(2):
        v = jnp.zeros((16, 256), jnp.int32)
        for b in range(4):
            v = jnp.where(lane == b, cit_ref[k, b], v)
        ids.append(v)
    second = (ids[0] == owner * 2 + 1) | (ids[1] == owner * 2 + 1)
    first = (ids[0] == owner * 2) | (ids[1] == owner * 2)
    cited = jnp.where(first | second, 1.0, 0.0).astype(F32)
    sel = jnp.where(second, 1.0, 0.0).astype(F32)
    sel = jnp.max(sel, axis=1, keepdims=True) + jnp.zeros((16, 256), F32)
    for t in range(NZ):
        for w in range(2):
            o = w * NZ + t
            info_out[t, w : w + 1, :] = cited[o : o + 1]
            info_out[t, 2 + w : 3 + w, :] = sel[o : o + 1]
        info_out[t, 4:8, :] = jnp.zeros((4, 256), F32)
    info_in[z] = info_out[z]
    pl.semaphore_wait(barrier, 12)

    def ag(direction, arr, t):
        if direction == 0:
            home, to = lax.rem(z - t + NZ, NZ), lax.rem(z + 1, NZ)
        else:
            home, to = lax.rem(z + t, NZ), lax.rem(z + NZ - 1, NZ)
        return remote(
            G.at[home, arr], G.at[home, arr],
            ag_send.at[direction, arr, t], ag_recv.at[direction, arr, t], at_z(to),
        )

    for direction in range(2):
        for arr in range(2):
            ag(direction, arr, 0).start()

    def info_copy(r):
        to = lax.rem(z + r, NZ)
        return remote(info_out.at[to], info_in.at[z], inf_send.at[r], inf_recv.at[r], at_z(to))

    def info_start(r, _):
        info_copy(r).start()
        return 0

    lax.fori_loop(1, NZ, info_start, 0)

    def relay(t):
        for direction in range(2):
            for arr in range(2):
                ag(direction, arr, t - 1).wait_recv()
                if t < 3 or direction == arr:
                    ag(direction, arr, t).start()

    out_row = lax.broadcasted_iota(jnp.int32, (256, 256), 0)
    in_row = lax.broadcasted_iota(jnp.int32, (256, 256), 1)
    PM[...] = jnp.where(in_row == (out_row % 64) * 4 + out_row // 64, 1.0, 0.0).astype(BF)

    def piece(k):
        w_load(k).wait()

        def sort(i, _):
            for u in range(4):
                b = i * 4 + u
                got = dot(PM[...], W32[k, pl.ds(pl.multiple_of(b * 256, 256), 256), :], NN).astype(BF)
                rows = pl.ds(pl.multiple_of(k * depth + b * 64, 64), 64)
                for n in range(4):
                    W[rows, n * HS : n * HS + HS] = got[n * 64 : n * 64 + 64]
            return 0

        lax.fori_loop(0, depth // 256, sort, 0)
        x_load(k).wait()
        rows = pl.ds(pl.multiple_of(k * depth, depth), depth)
        acc[...] += dot(X[k], W[rows, :], NN)

    def piece_loop(k, _):
        piece(k)
        return 0

    def kv_copy(h):
        return remote(KV.at[yh, h], KV.at[yh, h], kv_send.at[h], kv_recv.at[h], y_mate)

    acc[...] = jnp.zeros_like(acc)
    lax.fori_loop(0, KC - 2, piece_loop, 0)
    relay(1)
    lax.fori_loop(KC - 2, KC, piece_loop, 0)
    for h in range(2):
        KV[yh, h] = acc[:, h * 256 : h * 256 + 256].astype(BF)
        kv_copy(h).start()

    def kv_wait(h):
        pltpu.make_async_remote_copy(
            src_ref=KV.at[1 - yh, h], dst_ref=KV.at[1 - yh, h], send_sem=kv_send.at[h],
            recv_sem=kv_recv.at[h], device_id=y_mate, device_id_type=pl.DeviceIdType.MESH,
        ).wait_recv()

    def info_wait(r, _):
        info_copy(r).wait_recv()
        return 0

    relay(2)
    lax.fori_loop(1, NZ, info_wait, 0)
    for h in range(2):
        kv_wait(h)

    def chosen(j, h):
        out = []
        for w in range(2):
            f = info_in[j, 2 + w : 3 + w, :] + jnp.zeros((CL, 256), F32)
            one, zero = f.astype(BF), (1.0 - f).astype(BF)
            out.append(KV[w, h, 0:CL, :] * zero + KV[w, h, CL : 2 * CL, :] * one)
        return jnp.concatenate(out, axis=0)

    def st_copy(j):
        r = lax.rem(j - z + NZ, NZ)
        return remote(st_out.at[j], st_in.at[z], st_send.at[r], st_recv.at[r], at_z(j))

    def att1(j):
        for h in range(2):
            kv = chosen(j, h)
            cols = slice(h * HS, h * HS + HS)
            sc = dot(kv[:, :HS], G[j, 0, :, cols], NT) * scaling
            sc = jnp.concatenate(
                [
                    jnp.where(info_in[j, w : w + 1, :] > 0.0, sc[w * CL : w * CL + CL], NEG)
                    for w in range(2)
                ],
                axis=0,
            )
            top = jnp.max(sc, axis=0, keepdims=True)
            e = jnp.exp(sc - top)
            dp = dot(kv[:, HS:], G[j, 1, :, cols], NT)
            E[j, h] = e
            DP[j, h] = dp
            st_out[j, 3 * h : 3 * h + 1, :] = top
            st_out[j, 3 * h + 1 : 3 * h + 2, :] = jnp.sum(e, axis=0, keepdims=True)
            st_out[j, 3 * h + 2 : 3 * h + 3, :] = jnp.sum(e * dp, axis=0, keepdims=True)
        st_out[j, 6:8, :] = jnp.zeros((2, 256), F32)

    def both(t):
        def side(i, _):
            j = lax.rem(z + NZ - t + 2 * i * t, NZ)
            att1(j)
            st_copy(j).start()
            return 0

        lax.fori_loop(0, 1 if t == 4 else 2, side, 0)

    att1(z)
    both(1)
    relay(3)
    both(2)
    both(3)
    ag(0, 0, 3).wait_recv()
    ag(1, 1, 3).wait_recv()
    both(4)

    st_in[z] = st_out[z]

    def st_wait(r, _):
        src = lax.rem(z + NZ - r, NZ)
        remote(st_out.at[src], st_in.at[src], st_send.at[r], st_recv.at[r], at_z(src)).wait_recv()
        return 0

    lax.fori_loop(1, NZ, st_wait, 0)
    for h in range(2):
        tops = [st_in[i, 3 * h : 3 * h + 1, :] for i in range(NZ)]
        top = functools.reduce(jnp.maximum, tops)
        total = jnp.zeros((1, 256), F32)
        dots = jnp.zeros((1, 256), F32)
        for i in range(NZ):
            f = jnp.exp(tops[i] - top)
            total += f * st_in[i, 3 * h + 1 : 3 * h + 2, :]
            dots += f * st_in[i, 3 * h + 2 : 3 * h + 3, :]
        res_out[3 * h : 3 * h + 1, :] = top
        res_out[3 * h + 1 : 3 * h + 2, :] = 1.0 / total
        res_out[3 * h + 2 : 3 * h + 3, :] = dots / total
    res_out[6:8, :] = jnp.zeros((2, 256), F32)
    res_in[z] = res_out[...]

    def res_copy(r):
        return remote(res_out, res_in.at[z], rs_send.at[r], rs_recv.at[r], at_z(lax.rem(z + r, NZ)))

    def res_start(r, _):
        res_copy(r).start()
        return 0

    lax.fori_loop(1, NZ, res_start, 0)
    GR[...] = jnp.zeros_like(GR)

    def at_copy(j):
        r = lax.rem(j - z + NZ, NZ)
        return remote(at_out.at[j], at_in.at[z], at_send.at[r], at_recv.at[r], at_z(j))

    def att2(r, _):
        j = lax.rem(z + NZ - r, NZ)

        @pl.when(r > 0)
        def _():
            remote(res_out, res_in.at[j], rs_send.at[r], rs_recv.at[r], at_z(j)).wait_recv()

        for h in range(2):
            cols = slice(h * HS, h * HS + HS)
            f = jnp.exp(st_out[j, 3 * h : 3 * h + 1, :] - res_in[j, 3 * h : 3 * h + 1, :])
            p = E[j, h] * (f * res_in[j, 3 * h + 1 : 3 * h + 2, :])
            rounded = p.astype(BF)
            ds = (p * (DP[j, h] - res_in[j, 3 * h + 2 : 3 * h + 3, :])).astype(BF)
            kg = dot(ds, G[j, 0, :, cols], NN) * scaling
            vg = dot(rounded, G[j, 1, :, cols], NN)
            part = jnp.concatenate([kg, vg], axis=1)
            for w in range(2):
                one = info_in[j, 2 + w : 3 + w, :]
                mine = part[w * CL : w * CL + CL]
                GR[w, 0:CL, h * 256 : h * 256 + 256] += mine * (1.0 - one)
                GR[w, CL : 2 * CL, h * 256 : h * 256 + 256] += mine * one
            values = chosen(j, h)[:, HS:]
            at_out[j, cols, :] = dot(values, rounded, TN).astype(BF)

        @pl.when(r > 0)
        def _():
            at_copy(j).start()

        return 0

    lax.fori_loop(0, NZ, att2, 0)
    at_in[z] = at_out[z]

    yg_out[...] = GR[1 - yh].astype(BF)
    yg = remote(yg_out, yg_in, yg_send, yg_recv, y_mate)
    yg.start()
    yg.wait_recv()
    kvg[...] = (GR[yh] + yg_in[...].astype(F32)).astype(BF)

    def w_rows(i, core):
        e = ((i // 2) * 2 + core) * 2 + i % 2
        return W[pl.ds(pl.multiple_of(e * 512, 512), 512), :]

    def cs_copy(i):
        return remote(cs_out.at[i], cs_in.at[i], cs_send.at[i], cs_recv.at[i], core_mate)

    def to_core(i, _):
        cs_out[i] = dot(kvg[...], w_rows(i, 1 - c), NT).astype(BF)
        cs_copy(i).start()
        return 0

    lax.fori_loop(0, 8, to_core, 0)

    def own_core(i, _):
        own = dot(kvg[...], w_rows(i, c), NT)
        cs_copy(i).wait_recv()
        R[i // 2, i % 2] = (own + cs_in[i].astype(F32)).astype(BF)
        return 0

    lax.fori_loop(0, 8, own_core, 0)

    two, nxt, prv = lax.rem(x + 2, NX), lax.rem(x + 1, NX), lax.rem(x + 3, NX)

    def xsum(src, tmp, into, ssem, rsem):
        def at(i, half):
            return src(i, slice(half * 256, half * 256 + 256))

        firsts = [
            remote(at(two, 0), into.at[0], ssem.at[0], rsem.at[0], x_right),
            remote(at(two, 1), into.at[1], ssem.at[1], rsem.at[1], x_left),
            remote(at(nxt, 1), into.at[2], ssem.at[2], rsem.at[2], x_right),
            remote(at(prv, 0), into.at[3], ssem.at[3], rsem.at[3], x_left),
        ]
        seconds = [
            remote(tmp.at[0], into.at[4], ssem.at[4], rsem.at[4], x_right),
            remote(tmp.at[1], into.at[5], ssem.at[5], rsem.at[5], x_left),
        ]

        def relay():
            for i, (to, half) in enumerate([(nxt, 0), (prv, 1)]):
                firsts[i].wait_recv()
                tmp[i] = (at(to, half)[...].astype(F32) + into[i].astype(F32)).astype(BF)
                seconds[i].start()

        def finish():
            firsts[2].wait_recv()
            firsts[3].wait_recv()
            seconds[0].wait_recv()
            seconds[1].wait_recv()
            halves = []
            for half, got in [(0, (4, 3)), (1, (2, 5))]:
                v = at(x, half)[...].astype(F32)
                for g in got:
                    v += into[g].astype(F32)
                halves.append(v)
            return halves

        def start():
            for cp in firsts:
                cp.start()

        def drain():
            for cp in firsts + seconds:
                cp.wait_send()

        return start, relay, finish, drain

    a_start, a_relay, a_finish, a_drain = xsum(
        lambda i, cols: R.at[i, :, 0:ROWS_A, cols], ax_tmp, ax_in, ax_send, ax_recv
    )
    b_start, b_relay, b_finish, b_drain = xsum(
        lambda i, cols: RB.at[i, :, cols], bx_tmp, bx_in, bx_send, bx_recv
    )
    by = remote(R.at[:, 1 - m, ROWS_A:256, :], by_in, by_send, by_recv, m_mate)
    a_start()
    by.start()
    a_relay()
    by.wait_recv()

    def add_b(i, _):
        RB[i] = (R[i, m, ROWS_A:256, :].astype(F32) + by_in[i].astype(F32)).astype(BF)
        return 0

    lax.fori_loop(0, NX, add_b, 0)
    b_start()
    fa = a_finish()
    for half in range(2):
        cols = slice(half * 256, half * 256 + 256)
        ay_out[:, :, cols] = fa[half].astype(BF)
    ay = remote(ay_out.at[1 - m], ay_in, ay_send, ay_recv, m_mate)
    ay.start()
    b_relay()

    def at_wait(r, _):
        src = lax.rem(z + NZ - r, NZ)
        remote(at_out.at[src], at_in.at[src], at_send.at[r], at_recv.at[r], at_z(src)).wait_recv()
        return 0

    lax.fori_loop(1, NZ, at_wait, 0)
    total = at_in[0].astype(F32)
    for i in range(1, NZ):
        total += at_in[i].astype(F32)
    att_ref[...] = total.T.astype(BF)

    fb = b_finish()
    for half in range(2):
        cols = slice(half * 256, half * 256 + 256)
        nbr_ref[ROWS_A:256, cols] = fb[half].astype(BF)
    ay.wait_recv()
    nbr_ref[0:ROWS_A, :] = (ay_out[m].astype(F32) + ay_in[...].astype(F32)).astype(BF)

    for direction in range(2):
        for arr in range(2):
            for t in range(4 if direction == arr else 3):
                ag(direction, arr, t).wait_send()
    for h in range(2):
        kv_copy(h).wait_send()

    def sent(r, _):
        j = lax.rem(z + r, NZ)
        info_copy(r).wait_send()
        st_copy(j).wait_send()
        res_copy(r).wait_send()
        at_copy(j).wait_send()
        return 0

    lax.fori_loop(1, NZ, sent, 0)
    yg.wait_send()

    def cs_sent(i, _):
        cs_copy(i).wait_send()
        return 0

    lax.fori_loop(0, 8, cs_sent, 0)
    by.wait_send()
    ay.wait_send()
    a_drain()
    b_drain()


def on_device(nbr_states, kv_weight, queries, out_grad, citations):
    width = kv_weight.shape[0]
    rest = 256 - ROWS_A
    weight = kv_weight.reshape(width, 2, 2, HS).transpose(0, 2, 1, 3).reshape(width * 4, HS)
    V, D = pltpu.VMEM, pltpu.SemaphoreType.DMA
    scratch = [
        V((KC, 256, width // KC), BF),
        V((KC, width * 4 // KC, HS), BF),
        V((width, 512), BF),
        V((256, 512), F32),
        V((NZ, 2, 256, 256), BF),
        V((2, 2, 256, 256), BF),
        V((NZ, 8, 256), F32),
        V((NZ, 8, 256), F32),
        V((NZ, 2, 256, 256), F32),
        V((NZ, 2, 256, 256), F32),
        V((NZ, 8, 256), F32),
        V((NZ, 8, 256), F32),
        V((8, 256), F32),
        V((NZ, 8, 256), F32),
        V((NZ, 256, 256), BF),
        V((NZ, 256, 256), BF),
        V((2, 256, 512), F32),
        V((256, 512), BF),
        V((256, 512), BF),
        V((256, 512), BF),
        V((8, 256, 512), BF),
        V((8, 256, 512), BF),
        V((NX, 2, 256, 512), BF),
        V((NX, rest, 512), BF),
        V((NX, rest, 512), BF),
        V((6, 2, ROWS_A, 256), BF),
        V((2, 2, ROWS_A, 256), BF),
        V((6, rest, 256), BF),
        V((2, rest, 256), BF),
        V((2, ROWS_A, 512), BF),
        V((ROWS_A, 512), BF),
        V((256, 256), BF),
        D((2, KC)),
        D((2, 2, 4)), D((2, 2, 4)),
        D((2,)), D((2,)),
        D((NZ,)), D((NZ,)),
        D((NZ,)), D((NZ,)),
        D((NZ,)), D((NZ,)),
        D((NZ,)), D((NZ,)),
        D, D,
        D((8,)), D((8,)),
        D, D,
        D((6,)), D((6,)),
        D((6,)), D((6,)),
        D, D,
    ]
    vmem = pl.BlockSpec(memory_space=pltpu.VMEM)
    hbm = pl.BlockSpec(memory_space=pl.ANY)
    return pl.pallas_call(
        kernel,
        out_shape=(
            jax.ShapeDtypeStruct((256, 256), BF),
            jax.ShapeDtypeStruct((256, 512), BF),
        ),
        in_specs=[pl.BlockSpec(memory_space=pltpu.SMEM), vmem, vmem, hbm, hbm],
        out_specs=(vmem, vmem),
        scratch_shapes=scratch,
        compiler_params=pltpu.CompilerParams(
            collective_id=0, has_side_effects=True, vmem_limit_bytes=56 * 2**20
        ),
        cost_estimate=pl.CostEstimate(
            flops=6 * 10**9, bytes_accessed=13 * 2**20, transcendentals=2 * 10**6
        ),
    )(citations.T, queries, out_grad, nbr_states, weight)


def solution(mesh):
    heads = ("section", "mp")
    return jax.shard_map(
        on_device,
        mesh=mesh,
        in_specs=(
            P("dp", None),
            P(None, None, heads),
            P("dp", heads),
            P("dp", heads),
            P("dp", None),
        ),
        out_specs=(P("dp", heads), P("dp", heads)),
        check_vma=False,
    )
```

```python
import functools

import jax
import jax.numpy as jnp
from jax import lax
from jax.experimental import pallas as pl
from jax.experimental.pallas import tpu as pltpu
from jax.sharding import PartitionSpec as P

HS = 128
CH = 64
CL = 128
NZ = 8
NX = 4
KC = 8
ROWS_A = 144
NEG = -1e30
BF = jnp.bfloat16
F32 = jnp.float32
NT = (((1,), (1,)), ((), ()))
NN = (((1,), (0,)), ((), ()))
TN = (((0,), (0,)), ((), ()))


def dot(a, b, dims):
    return lax.dot_general(a, b, dims, preferred_element_type=F32)


def kernel(
    cit_ref, q_ref, g_ref, x_hbm, w_hbm, att_ref, nbr_ref,
    X, W32, W, acc, G, KV, info_out, info_in, E, DP, st_out, st_in, res_out, res_in,
    at_out, at_in, GR, yg_out, yg_in, kvg, cs_out, cs_in, R, by_in, RB,
    ax_in, ax_tmp, bx_in, bx_tmp, ay_out, ay_in, PM,
    ld_sem, ag_send, ag_recv, kv_send, kv_recv, inf_send, inf_recv, st_send, st_recv,
    rs_send, rs_recv, at_send, at_recv, yg_send, yg_recv, cs_send, cs_recv,
    by_send, by_recv, ax_send, ax_recv, bx_send, bx_recv, ay_send, ay_recv,
):
    s, d, m = lax.axis_index("section"), lax.axis_index("dp"), lax.axis_index("mp")
    x, c = s // 2, s % 2
    yh, z = d // NZ, d % NZ
    depth = x_hbm.shape[1] // KC
    scaling = 1.0 / HS**0.5

    def at_z(zt):
        return {"dp": yh * NZ + zt}

    y_mate = {"dp": (1 - yh) * NZ + z}
    core_mate = {"section": x * 2 + (1 - c)}
    x_right = {"section": lax.rem(x + 1, NX) * 2 + c}
    x_left = {"section": lax.rem(x + NX - 1, NX) * 2 + c}
    m_mate = {"mp": 1 - m}

    def remote(src, dst, ssem, rsem, dev):
        return pltpu.make_async_remote_copy(
            src_ref=src, dst_ref=dst, send_sem=ssem, recv_sem=rsem,
            device_id=dev, device_id_type=pl.DeviceIdType.MESH,
        )

    def x_load(k):
        return pltpu.make_async_copy(
            x_hbm.at[:, pl.ds(pl.multiple_of(k * depth, depth), depth)], X.at[k], ld_sem.at[1, k]
        )

    def w_load(k):
        return pltpu.make_async_copy(
            w_hbm.at[pl.ds(pl.multiple_of(k * 4 * depth, depth), 4 * depth), :], W32.at[k], ld_sem.at[0, k]
        )

    def start_loads(k, _):
        w_load(k).start()
        x_load(k).start()
        return 0

    lax.fori_loop(0, KC, start_loads, 0)

    barrier = pltpu.get_barrier_semaphore()
    for dev in [at_z(lax.rem(z + r, NZ)) for r in range(1, NZ)] + [
        y_mate, core_mate, x_right, x_left, m_mate
    ]:
        pl.semaphore_signal(barrier, inc=1, device_id=dev, device_id_type=pl.DeviceIdType.MESH)

    G[z, 0] = q_ref[...]
    G[z, 1] = g_ref[...]
    lane = lax.broadcasted_iota(jnp.int32, (16, 256), 1) // CH
    owner = lax.broadcasted_iota(jnp.int32, (16, 256), 0)
    ids = []
    for k in range(2):
        v = jnp.zeros((16, 256), jnp.int32)
        for b in range(4):
            v = jnp.where(lane == b, cit_ref[k, b], v)
        ids.append(v)
    second = (ids[0] == owner * 2 + 1) | (ids[1] == owner * 2 + 1)
    first = (ids[0] == owner * 2) | (ids[1] == owner * 2)
    cited = jnp.where(first | second, 1.0, 0.0).astype(F32)
    sel = jnp.where(second, 1.0, 0.0).astype(F32)
    sel = jnp.max(sel, axis=1, keepdims=True) + jnp.zeros((16, 256), F32)
    for t in range(NZ):
        for w in range(2):
            o = w * NZ + t
            info_out[t, w : w + 1, :] = cited[o : o + 1]
            info_out[t, 2 + w : 3 + w, :] = sel[o : o + 1]
        info_out[t, 4:8, :] = jnp.zeros((4, 256), F32)
    info_in[z] = info_out[z]
    pl.semaphore_wait(barrier, 12)

    def ag(direction, u, t):
        if direction == 0:
            home, to, arr = lax.rem(z - t + NZ, NZ), lax.rem(z + 1, NZ), u // 2
        else:
            home, to, arr = lax.rem(z + t, NZ), lax.rem(z + NZ - 1, NZ), 1 - u // 2
        piece = G.at[home, arr, pl.ds(pl.multiple_of((u % 2) * 128, 128), 128)]
        return remote(piece, piece, ag_send.at[direction, u, t], ag_recv.at[direction, u, t], at_z(to))

    for u in range(4):
        for direction in range(2):
            ag(direction, u, 0).start()

    def info_copy(r):
        to = lax.rem(z + r, NZ)
        return remote(info_out.at[to], info_in.at[z], inf_send.at[r], inf_recv.at[r], at_z(to))

    def info_start(r, _):
        info_copy(r).start()
        return 0

    lax.fori_loop(1, NZ, info_start, 0)

    def relay(t, u):
        for direction in range(2):
            ag(direction, u, t - 1).wait_recv()
            ag(direction, u, t).start()

    def arrived(t, u):
        for direction in range(2):
            ag(direction, u, t).wait_recv()

    out_row = lax.broadcasted_iota(jnp.int32, (256, 256), 0)
    in_row = lax.broadcasted_iota(jnp.int32, (256, 256), 1)
    PM[...] = jnp.where(in_row == (out_row % 64) * 4 + out_row // 64, 1.0, 0.0).astype(BF)

    def piece(k, _):
        w_load(k).wait()

        def sort(i, _):
            for u in range(4):
                b = i * 4 + u
                got = dot(PM[...], W32[k, pl.ds(pl.multiple_of(b * 256, 256), 256), :], NN).astype(BF)
                rows = pl.ds(pl.multiple_of(k * depth + b * 64, 64), 64)
                for n in range(4):
                    W[rows, n * HS : n * HS + HS] = got[n * 64 : n * 64 + 64]
            return 0

        lax.fori_loop(0, depth // 256, sort, 0)
        x_load(k).wait()
        rows = pl.ds(pl.multiple_of(k * depth, depth), depth)
        acc[...] += dot(X[k], W[rows, 0:256], NN)

        @pl.when(k >= 2)
        def _():
            relay(1 + (k - 2) // 4, (k - 2) % 4)

        return 0

    def piece_1(k, _):
        rows = pl.ds(pl.multiple_of(k * depth, depth), depth)
        acc[...] += dot(X[k], W[rows, 256:512], NN)
        return 0

    def kv_copy(h):
        return remote(KV.at[yh, h], KV.at[yh, h], kv_send.at[h], kv_recv.at[h], y_mate)

    for h, body in enumerate([piece, piece_1]):
        acc[...] = jnp.zeros_like(acc)
        lax.fori_loop(0, KC, body, 0)
        KV[yh, h] = acc[...].astype(BF)
        kv_copy(h).start()

    def kv_wait(h):
        pltpu.make_async_remote_copy(
            src_ref=KV.at[1 - yh, h], dst_ref=KV.at[1 - yh, h], send_sem=kv_send.at[h],
            recv_sem=kv_recv.at[h], device_id=y_mate, device_id_type=pl.DeviceIdType.MESH,
        ).wait_recv()

    def info_wait(r, _):
        info_copy(r).wait_recv()
        return 0

    relay(2, 2)
    relay(2, 3)
    lax.fori_loop(1, NZ, info_wait, 0)
    relay(3, 0)
    for h in range(2):
        kv_wait(h)

    def chosen(j, h):
        out = []
        for w in range(2):
            f = info_in[j, 2 + w : 3 + w, :] + jnp.zeros((CL, 256), F32)
            one, zero = f.astype(BF), (1.0 - f).astype(BF)
            out.append(KV[w, h, 0:CL, :] * zero + KV[w, h, CL : 2 * CL, :] * one)
        return jnp.concatenate(out, axis=0)

    def st_copy(j):
        r = lax.rem(j - z + NZ, NZ)
        return remote(st_out.at[j], st_in.at[z], st_send.at[r], st_recv.at[r], at_z(j))

    def att1(j):
        for h in range(2):
            kv = chosen(j, h)
            cols = slice(h * HS, h * HS + HS)
            sc = dot(kv[:, :HS], G[j, 0, :, cols], NT) * scaling
            sc = jnp.concatenate(
                [
                    jnp.where(info_in[j, w : w + 1, :] > 0.0, sc[w * CL : w * CL + CL], NEG)
                    for w in range(2)
                ],
                axis=0,
            )
            top = jnp.max(sc, axis=0, keepdims=True)
            e = jnp.exp(sc - top)
            dp = dot(kv[:, HS:], G[j, 1, :, cols], NT)
            E[j, h] = e
            DP[j, h] = dp
            st_out[j, 3 * h : 3 * h + 1, :] = top
            st_out[j, 3 * h + 1 : 3 * h + 2, :] = jnp.sum(e, axis=0, keepdims=True)
            st_out[j, 3 * h + 2 : 3 * h + 3, :] = jnp.sum(e * dp, axis=0, keepdims=True)
        st_out[j, 6:8, :] = jnp.zeros((2, 256), F32)

    def both(t):
        def side(i, _):
            j = lax.rem(z + NZ - t + 2 * i * t, NZ)
            att1(j)
            st_copy(j).start()
            return 0

        lax.fori_loop(0, 1 if t == 4 else 2, side, 0)

    relay(3, 1)
    att1(z)
    both(1)
    both(2)
    arrived(2, 2)
    arrived(2, 3)
    both(3)
    arrived(3, 0)
    arrived(3, 1)
    both(4)

    st_in[z] = st_out[z]

    def st_wait(r, _):
        src = lax.rem(z + NZ - r, NZ)
        remote(st_out.at[src], st_in.at[src], st_send.at[r], st_recv.at[r], at_z(src)).wait_recv()
        return 0

    lax.fori_loop(1, NZ, st_wait, 0)
    for h in range(2):
        tops = [st_in[i, 3 * h : 3 * h + 1, :] for i in range(NZ)]
        top = functools.reduce(jnp.maximum, tops)
        total = jnp.zeros((1, 256), F32)
        dots = jnp.zeros((1, 256), F32)
        for i in range(NZ):
            f = jnp.exp(tops[i] - top)
            total += f * st_in[i, 3 * h + 1 : 3 * h + 2, :]
            dots += f * st_in[i, 3 * h + 2 : 3 * h + 3, :]
        res_out[3 * h : 3 * h + 1, :] = top
        res_out[3 * h + 1 : 3 * h + 2, :] = 1.0 / total
        res_out[3 * h + 2 : 3 * h + 3, :] = dots / total
    res_out[6:8, :] = jnp.zeros((2, 256), F32)
    res_in[z] = res_out[...]

    def res_copy(r):
        return remote(res_out, res_in.at[z], rs_send.at[r], rs_recv.at[r], at_z(lax.rem(z + r, NZ)))

    def res_start(r, _):
        res_copy(r).start()
        return 0

    lax.fori_loop(1, NZ, res_start, 0)
    GR[...] = jnp.zeros_like(GR)

    def at_copy(j):
        r = lax.rem(j - z + NZ, NZ)
        return remote(at_out.at[j], at_in.at[z], at_send.at[r], at_recv.at[r], at_z(j))

    def att2(r, _):
        j = lax.rem(z + NZ - r, NZ)

        @pl.when(r > 0)
        def _():
            remote(res_out, res_in.at[j], rs_send.at[r], rs_recv.at[r], at_z(j)).wait_recv()

        for h in range(2):
            cols = slice(h * HS, h * HS + HS)
            f = jnp.exp(st_out[j, 3 * h : 3 * h + 1, :] - res_in[j, 3 * h : 3 * h + 1, :])
            p = E[j, h] * (f * res_in[j, 3 * h + 1 : 3 * h + 2, :])
            rounded = p.astype(BF)
            ds = (p * (DP[j, h] - res_in[j, 3 * h + 2 : 3 * h + 3, :])).astype(BF)
            kg = dot(ds, G[j, 0, :, cols], NN) * scaling
            vg = dot(rounded, G[j, 1, :, cols], NN)
            part = jnp.concatenate([kg, vg], axis=1)
            for w in range(2):
                one = info_in[j, 2 + w : 3 + w, :]
                mine = part[w * CL : w * CL + CL]
                GR[w, 0:CL, h * 256 : h * 256 + 256] += mine * (1.0 - one)
                GR[w, CL : 2 * CL, h * 256 : h * 256 + 256] += mine * one
            values = chosen(j, h)[:, HS:]
            at_out[j, cols, :] = dot(values, rounded, TN).astype(BF)
        return 0

    lax.fori_loop(0, NZ, att2, 0)
    at_in[z] = at_out[z]

    yg_out[...] = GR[1 - yh].astype(BF)
    yg = remote(yg_out, yg_in, yg_send, yg_recv, y_mate)
    yg.start()

    def at_start(r, _):
        at_copy(lax.rem(z + r, NZ)).start()
        return 0

    lax.fori_loop(1, NZ, at_start, 0)
    yg.wait_recv()
    kvg[...] = (GR[yh] + yg_in[...].astype(F32)).astype(BF)

    two, nxt, prv = lax.rem(x + 2, NX), lax.rem(x + 1, NX), lax.rem(x + 3, NX)
    order = [two, nxt, prv, x]

    def product(n, core, yl):
        e = (order[n] * 2 + core) * 2 + yl
        return dot(kvg[...], W[pl.ds(pl.multiple_of(e * 512, 512), 512), :], NT)

    def cs_copy(n, yl):
        return remote(cs_out.at[n, yl], cs_in.at[n, yl], cs_send.at[n, yl], cs_recv.at[n, yl], core_mate)

    def for_mate(n):
        def one(yl, _):
            cs_out[n, yl] = product(n, 1 - c, yl).astype(BF)
            cs_copy(n, yl).start()
            return 0

        lax.fori_loop(0, 2, one, 0)

    def by_copy(n):
        return remote(R.at[n, 1 - m, ROWS_A:256, :], by_in.at[n], by_send.at[n], by_recv.at[n], m_mate)

    def own(n):
        def one(yl, _):
            mine = product(n, c, yl)
            cs_copy(n, yl).wait_recv()
            R[n, yl] = (mine + cs_in[n, yl].astype(F32)).astype(BF)
            return 0

        lax.fori_loop(0, 2, one, 0)
        by_copy(n).start()

    def xsum(src, tmp, into, ssem, rsem):
        def at(n, half):
            return src(n, slice(half * 256, half * 256 + 256))

        firsts = [
            remote(at(0, 0), into.at[0], ssem.at[0], rsem.at[0], x_right),
            remote(at(0, 1), into.at[1], ssem.at[1], rsem.at[1], x_left),
            remote(at(1, 1), into.at[2], ssem.at[2], rsem.at[2], x_right),
            remote(at(2, 0), into.at[3], ssem.at[3], rsem.at[3], x_left),
        ]
        seconds = [
            remote(tmp.at[0], into.at[4], ssem.at[4], rsem.at[4], x_right),
            remote(tmp.at[1], into.at[5], ssem.at[5], rsem.at[5], x_left),
        ]

        def start(n):
            for i in [(0, 1), (2,), (3,), ()][n]:
                firsts[i].start()

        def relay():
            for i in range(2):
                firsts[i].wait_recv()
                tmp[i] = (at(1 + i, i)[...].astype(F32) + into[i].astype(F32)).astype(BF)
                seconds[i].start()

        def finish():
            firsts[2].wait_recv()
            firsts[3].wait_recv()
            seconds[0].wait_recv()
            seconds[1].wait_recv()
            halves = []
            for half, got in [(0, (4, 3)), (1, (2, 5))]:
                v = at(3, half)[...].astype(F32)
                for g in got:
                    v += into[g].astype(F32)
                halves.append(v)
            return halves

        def drain():
            for cp in firsts + seconds:
                cp.wait_send()

        return start, relay, finish, drain

    a_start, a_relay, a_finish, a_drain = xsum(
        lambda n, cols: R.at[n, :, 0:ROWS_A, cols], ax_tmp, ax_in, ax_send, ax_recv
    )
    b_start, b_relay, b_finish, b_drain = xsum(
        lambda n, cols: RB.at[n, :, cols], bx_tmp, bx_in, bx_send, bx_recv
    )

    def add_b(n):
        by_copy(n).wait_recv()
        RB[n] = (R[n, m, ROWS_A:256, :].astype(F32) + by_in[n].astype(F32)).astype(BF)
        b_start(n)

    for_mate(0)
    for_mate(1)
    own(0)
    a_start(0)
    for_mate(2)
    own(1)
    a_start(1)
    for_mate(3)
    own(2)
    a_start(2)
    a_relay()
    own(3)
    for n in range(NX):
        add_b(n)
    fa = a_finish()
    for half in range(2):
        cols = slice(half * 256, half * 256 + 256)
        ay_out[:, :, cols] = fa[half].astype(BF)
    ay = remote(ay_out.at[1 - m], ay_in, ay_send, ay_recv, m_mate)
    ay.start()
    b_relay()

    def at_wait(r, _):
        src = lax.rem(z + NZ - r, NZ)
        remote(at_out.at[src], at_in.at[src], at_send.at[r], at_recv.at[r], at_z(src)).wait_recv()
        return 0

    lax.fori_loop(1, NZ, at_wait, 0)
    total = at_in[0].astype(F32)
    for i in range(1, NZ):
        total += at_in[i].astype(F32)
    att_ref[...] = total.T.astype(BF)

    fb = b_finish()
    for half in range(2):
        cols = slice(half * 256, half * 256 + 256)
        nbr_ref[ROWS_A:256, cols] = fb[half].astype(BF)
    ay.wait_recv()
    nbr_ref[0:ROWS_A, :] = (ay_out[m].astype(F32) + ay_in[...].astype(F32)).astype(BF)

    for direction in range(2):
        for u in range(4):
            for t in range(4 if u < 2 else 3):
                ag(direction, u, t).wait_send()
    for h in range(2):
        kv_copy(h).wait_send()

    def sent(r, _):
        j = lax.rem(z + r, NZ)
        info_copy(r).wait_send()
        st_copy(j).wait_send()
        res_copy(r).wait_send()
        at_copy(j).wait_send()
        return 0

    lax.fori_loop(1, NZ, sent, 0)
    yg.wait_send()

    for n in range(NX):
        for yl in range(2):
            cs_copy(n, yl).wait_send()
        by_copy(n).wait_send()
    ay.wait_send()
    a_drain()
    b_drain()


def on_device(nbr_states, kv_weight, queries, out_grad, citations):
    width = kv_weight.shape[0]
    rest = 256 - ROWS_A
    weight = kv_weight.reshape(width, 2, 2, HS).transpose(0, 2, 1, 3).reshape(width * 4, HS)
    V, D = pltpu.VMEM, pltpu.SemaphoreType.DMA
    scratch = [
        V((KC, 256, width // KC), BF),
        V((KC, width * 4 // KC, HS), BF),
        V((width, 512), BF),
        V((256, 256), F32),
        V((NZ, 2, 256, 256), BF),
        V((2, 2, 256, 256), BF),
        V((NZ, 8, 256), F32),
        V((NZ, 8, 256), F32),
        V((NZ, 2, 256, 256), F32),
        V((NZ, 2, 256, 256), F32),
        V((NZ, 8, 256), F32),
        V((NZ, 8, 256), F32),
        V((8, 256), F32),
        V((NZ, 8, 256), F32),
        V((NZ, 256, 256), BF),
        V((NZ, 256, 256), BF),
        V((2, 256, 512), F32),
        V((256, 512), BF),
        V((256, 512), BF),
        V((256, 512), BF),
        V((NX, 2, 256, 512), BF),
        V((NX, 2, 256, 512), BF),
        V((NX, 2, 256, 512), BF),
        V((NX, rest, 512), BF),
        V((NX, rest, 512), BF),
        V((6, 2, ROWS_A, 256), BF),
        V((2, 2, ROWS_A, 256), BF),
        V((6, rest, 256), BF),
        V((2, rest, 256), BF),
        V((2, ROWS_A, 512), BF),
        V((ROWS_A, 512), BF),
        V((256, 256), BF),
        D((2, KC)),
        D((2, 4, 4)), D((2, 4, 4)),
        D((2,)), D((2,)),
        D((NZ,)), D((NZ,)),
        D((NZ,)), D((NZ,)),
        D((NZ,)), D((NZ,)),
        D((NZ,)), D((NZ,)),
        D, D,
        D((NX, 2)), D((NX, 2)),
        D((NX,)), D((NX,)),
        D((6,)), D((6,)),
        D((6,)), D((6,)),
        D, D,
    ]
    vmem = pl.BlockSpec(memory_space=pltpu.VMEM)
    hbm = pl.BlockSpec(memory_space=pl.ANY)
    return pl.pallas_call(
        kernel,
        out_shape=(
            jax.ShapeDtypeStruct((256, 256), BF),
            jax.ShapeDtypeStruct((256, 512), BF),
        ),
        in_specs=[pl.BlockSpec(memory_space=pltpu.SMEM), vmem, vmem, hbm, hbm],
        out_specs=(vmem, vmem),
        scratch_shapes=scratch,
        compiler_params=pltpu.CompilerParams(
            collective_id=0, has_side_effects=True, vmem_limit_bytes=56 * 2**20
        ),
        cost_estimate=pl.CostEstimate(
            flops=6 * 10**9, bytes_accessed=13 * 2**20, transcendentals=2 * 10**6
        ),
    )(citations.T, queries, out_grad, nbr_states, weight)


def solution(mesh):
    heads = ("section", "mp")
    return jax.shard_map(
        on_device,
        mesh=mesh,
        in_specs=(
            P("dp", None),
            P(None, None, heads),
            P("dp", heads),
            P("dp", heads),
            P("dp", None),
        ),
        out_specs=(P("dp", heads), P("dp", heads)),
        check_vma=False,
    )
```

```python
import functools

import jax
import jax.numpy as jnp
from jax import lax
from jax.experimental import pallas as pl
from jax.experimental.pallas import tpu as pltpu
from jax.sharding import PartitionSpec as P

HS = 128
CH = 64
CL = 128
NZ = 8
NX = 4
KC = 8
ROWS_A = 144
NEG = -1e30
BF = jnp.bfloat16
F32 = jnp.float32
NT = (((1,), (1,)), ((), ()))
NN = (((1,), (0,)), ((), ()))
TN = (((0,), (0,)), ((), ()))


def dot(a, b, dims):
    return lax.dot_general(a, b, dims, preferred_element_type=F32)


def kernel(
    cit_ref, q_hbm, g_hbm, x_hbm, w_hbm, att_ref, nbr_ref,
    X, W32, W, acc, G, KV, info_out, info_in, E, DP, st_out, st_in, res_out, res_in,
    at_out, at_in, GR, yg_out, yg_in, kvg, cs_out, cs_in, R, by_in, RB,
    ax_in, ax_tmp, bx_in, bx_tmp, ay_out, ay_in, PM,
    ld_sem, own_sem, ag_send, ag_recv, kv_send, kv_recv, inf_send, inf_recv, st_send, st_recv,
    rs_send, rs_recv, at_send, at_recv, yg_send, yg_recv, cs_send, cs_recv,
    by_send, by_recv, ax_send, ax_recv, bx_send, bx_recv, ay_send, ay_recv,
):
    s, d, m = lax.axis_index("section"), lax.axis_index("dp"), lax.axis_index("mp")
    x, c = s // 2, s % 2
    yh, z = d // NZ, d % NZ
    depth = x_hbm.shape[1] // KC
    scaling = 1.0 / HS**0.5

    def at_z(zt):
        return {"dp": yh * NZ + zt}

    y_mate = {"dp": (1 - yh) * NZ + z}
    core_mate = {"section": x * 2 + (1 - c)}
    x_right = {"section": lax.rem(x + 1, NX) * 2 + c}
    x_left = {"section": lax.rem(x + NX - 1, NX) * 2 + c}
    m_mate = {"mp": 1 - m}

    def remote(src, dst, ssem, rsem, dev):
        return pltpu.make_async_remote_copy(
            src_ref=src, dst_ref=dst, send_sem=ssem, recv_sem=rsem,
            device_id=dev, device_id_type=pl.DeviceIdType.MESH,
        )

    def x_load(k):
        return pltpu.make_async_copy(
            x_hbm.at[:, pl.ds(pl.multiple_of(k * depth, depth), depth)], X.at[k], ld_sem.at[1, k]
        )

    def w_load(k):
        return pltpu.make_async_copy(
            w_hbm.at[pl.ds(pl.multiple_of(k * 4 * depth, depth), 4 * depth), :], W32.at[k], ld_sem.at[0, k]
        )

    own_rows = [pltpu.make_async_copy(src, G.at[z, i], own_sem.at[i]) for i, src in enumerate([q_hbm, g_hbm])]
    for cp in own_rows:
        cp.start()

    def start_loads(k, _):
        w_load(k).start()
        x_load(k).start()
        return 0

    lax.fori_loop(0, KC, start_loads, 0)

    barrier = pltpu.get_barrier_semaphore()
    for dev in [at_z(lax.rem(z + r, NZ)) for r in range(1, NZ)] + [
        y_mate, core_mate, x_right, x_left, m_mate
    ]:
        pl.semaphore_signal(barrier, inc=1, device_id=dev, device_id_type=pl.DeviceIdType.MESH)

    lane = lax.broadcasted_iota(jnp.int32, (16, 256), 1) // CH
    owner = lax.broadcasted_iota(jnp.int32, (16, 256), 0)
    ids = []
    for k in range(2):
        v = jnp.zeros((16, 256), jnp.int32)
        for b in range(4):
            v = jnp.where(lane == b, cit_ref[k, b], v)
        ids.append(v)
    second = (ids[0] == owner * 2 + 1) | (ids[1] == owner * 2 + 1)
    first = (ids[0] == owner * 2) | (ids[1] == owner * 2)
    cited = jnp.where(first | second, 1.0, 0.0).astype(F32)
    sel = jnp.where(second, 1.0, 0.0).astype(F32)
    sel = jnp.max(sel, axis=1, keepdims=True) + jnp.zeros((16, 256), F32)
    for t in range(NZ):
        for w in range(2):
            o = w * NZ + t
            info_out[t, w : w + 1, :] = cited[o : o + 1]
            info_out[t, 2 + w : 3 + w, :] = sel[o : o + 1]
        info_out[t, 4:8, :] = jnp.zeros((4, 256), F32)
    info_in[z] = info_out[z]
    for cp in own_rows:
        cp.wait()
    pl.semaphore_wait(barrier, 12)

    def ag(direction, u, t):
        if direction == 0:
            home, to, arr = lax.rem(z - t + NZ, NZ), lax.rem(z + 1, NZ), u // 2
        else:
            home, to, arr = lax.rem(z + t, NZ), lax.rem(z + NZ - 1, NZ), 1 - u // 2
        piece = G.at[home, arr, pl.ds(pl.multiple_of((u % 2) * 128, 128), 128)]
        return remote(piece, piece, ag_send.at[direction, u, t], ag_recv.at[direction, u, t], at_z(to))

    for u in range(4):
        for direction in range(2):
            ag(direction, u, 0).start()

    def info_copy(r):
        to = lax.rem(z + r, NZ)
        return remote(info_out.at[to], info_in.at[z], inf_send.at[r], inf_recv.at[r], at_z(to))

    def info_start(r, _):
        info_copy(r).start()
        return 0

    lax.fori_loop(1, NZ, info_start, 0)

    def relay(t, u):
        for direction in range(2):
            ag(direction, u, t - 1).wait_recv()
            ag(direction, u, t).start()

    def arrived(t, u):
        for direction in range(2):
            ag(direction, u, t).wait_recv()

    out_row = lax.broadcasted_iota(jnp.int32, (256, 256), 0)
    in_row = lax.broadcasted_iota(jnp.int32, (256, 256), 1)
    PM[...] = jnp.where(in_row == (out_row % 64) * 4 + out_row // 64, 1.0, 0.0).astype(BF)

    def piece(k, _):
        w_load(k).wait()

        def sort(i, _):
            for u in range(4):
                b = i * 4 + u
                got = dot(PM[...], W32[k, pl.ds(pl.multiple_of(b * 256, 256), 256), :], NN).astype(BF)
                rows = pl.ds(pl.multiple_of(k * depth + b * 64, 64), 64)
                for n in range(4):
                    W[rows, n * HS : n * HS + HS] = got[n * 64 : n * 64 + 64]
            return 0

        lax.fori_loop(0, depth // 256, sort, 0)
        x_load(k).wait()
        rows = pl.ds(pl.multiple_of(k * depth, depth), depth)
        acc[...] += dot(X[k], W[rows, 0:256], NN)

        @pl.when(k >= 2)
        def _():
            relay(1 + (k - 2) // 4, (k - 2) % 4)

        return 0

    def piece_1(k, _):
        rows = pl.ds(pl.multiple_of(k * depth, depth), depth)
        acc[...] += dot(X[k], W[rows, 256:512], NN)
        return 0

    def kv_copy(h):
        return remote(KV.at[yh, h], KV.at[yh, h], kv_send.at[h], kv_recv.at[h], y_mate)

    for h, body in enumerate([piece, piece_1]):
        acc[...] = jnp.zeros_like(acc)
        lax.fori_loop(0, KC, body, 0)
        KV[yh, h] = acc[...].astype(BF)
        kv_copy(h).start()

    def kv_wait(h):
        pltpu.make_async_remote_copy(
            src_ref=KV.at[1 - yh, h], dst_ref=KV.at[1 - yh, h], send_sem=kv_send.at[h],
            recv_sem=kv_recv.at[h], device_id=y_mate, device_id_type=pl.DeviceIdType.MESH,
        ).wait_recv()

    def info_wait(r, _):
        info_copy(r).wait_recv()
        return 0

    relay(2, 2)
    relay(2, 3)
    lax.fori_loop(1, NZ, info_wait, 0)
    relay(3, 0)
    relay(3, 1)
    for h in range(2):
        kv_wait(h)

    def chosen(j, h):
        out = []
        for w in range(2):
            f = info_in[j, 2 + w : 3 + w, :] + jnp.zeros((CL, 256), F32)
            one, zero = f.astype(BF), (1.0 - f).astype(BF)
            out.append(KV[w, h, 0:CL, :] * zero + KV[w, h, CL : 2 * CL, :] * one)
        return jnp.concatenate(out, axis=0)

    def st_copy(j):
        r = lax.rem(j - z + NZ, NZ)
        return remote(st_out.at[j], st_in.at[z], st_send.at[r], st_recv.at[r], at_z(j))

    def att1(j):
        for h in range(2):
            kv = chosen(j, h)
            cols = slice(h * HS, h * HS + HS)
            sc = dot(kv[:, :HS], G[j, 0, :, cols], NT) * scaling
            sc = jnp.concatenate(
                [
                    jnp.where(info_in[j, w : w + 1, :] > 0.0, sc[w * CL : w * CL + CL], NEG)
                    for w in range(2)
                ],
                axis=0,
            )
            top = jnp.max(sc, axis=0, keepdims=True)
            e = jnp.exp(sc - top)
            dp = dot(kv[:, HS:], G[j, 1, :, cols], NT)
            E[j, h] = e
            DP[j, h] = dp
            st_out[j, 3 * h : 3 * h + 1, :] = top
            st_out[j, 3 * h + 1 : 3 * h + 2, :] = jnp.sum(e, axis=0, keepdims=True)
            st_out[j, 3 * h + 2 : 3 * h + 3, :] = jnp.sum(e * dp, axis=0, keepdims=True)
        st_out[j, 6:8, :] = jnp.zeros((2, 256), F32)

    def both(t):
        def side(i, _):
            j = lax.rem(z + NZ - t + 2 * i * t, NZ)
            att1(j)
            st_copy(j).start()
            return 0

        lax.fori_loop(0, 1 if t == 4 else 2, side, 0)

    att1(z)
    both(1)
    both(2)
    arrived(2, 2)
    arrived(2, 3)
    both(3)
    arrived(3, 0)
    arrived(3, 1)
    both(4)

    st_in[z] = st_out[z]

    def st_wait(r, _):
        src = lax.rem(z + NZ - r, NZ)
        remote(st_out.at[src], st_in.at[src], st_send.at[r], st_recv.at[r], at_z(src)).wait_recv()
        return 0

    lax.fori_loop(1, NZ, st_wait, 0)
    for h in range(2):
        tops = [st_in[i, 3 * h : 3 * h + 1, :] for i in range(NZ)]
        top = functools.reduce(jnp.maximum, tops)
        total = jnp.zeros((1, 256), F32)
        dots = jnp.zeros((1, 256), F32)
        for i in range(NZ):
            f = jnp.exp(tops[i] - top)
            total += f * st_in[i, 3 * h + 1 : 3 * h + 2, :]
            dots += f * st_in[i, 3 * h + 2 : 3 * h + 3, :]
        res_out[3 * h : 3 * h + 1, :] = top
        res_out[3 * h + 1 : 3 * h + 2, :] = 1.0 / total
        res_out[3 * h + 2 : 3 * h + 3, :] = dots / total
    res_out[6:8, :] = jnp.zeros((2, 256), F32)
    res_in[z] = res_out[...]

    def res_copy(r):
        return remote(res_out, res_in.at[z], rs_send.at[r], rs_recv.at[r], at_z(lax.rem(z + r, NZ)))

    def res_start(r, _):
        res_copy(r).start()
        return 0

    lax.fori_loop(1, NZ, res_start, 0)
    GR[...] = jnp.zeros_like(GR)

    def at_copy(j):
        r = lax.rem(j - z + NZ, NZ)
        return remote(at_out.at[j], at_in.at[z], at_send.at[r], at_recv.at[r], at_z(j))

    def att2(r, _):
        j = lax.rem(z + NZ - r, NZ)

        @pl.when(r > 0)
        def _():
            remote(res_out, res_in.at[j], rs_send.at[r], rs_recv.at[r], at_z(j)).wait_recv()

        for h in range(2):
            cols = slice(h * HS, h * HS + HS)
            f = jnp.exp(st_out[j, 3 * h : 3 * h + 1, :] - res_in[j, 3 * h : 3 * h + 1, :])
            p = E[j, h] * (f * res_in[j, 3 * h + 1 : 3 * h + 2, :])
            rounded = p.astype(BF)
            ds = (p * (DP[j, h] - res_in[j, 3 * h + 2 : 3 * h + 3, :])).astype(BF)
            kg = dot(ds, G[j, 0, :, cols], NN) * scaling
            vg = dot(rounded, G[j, 1, :, cols], NN)
            part = jnp.concatenate([kg, vg], axis=1)
            for w in range(2):
                one = info_in[j, 2 + w : 3 + w, :]
                mine = part[w * CL : w * CL + CL]
                GR[w, 0:CL, h * 256 : h * 256 + 256] += mine * (1.0 - one)
                GR[w, CL : 2 * CL, h * 256 : h * 256 + 256] += mine * one
            values = chosen(j, h)[:, HS:]
            at_out[j, cols, :] = dot(values, rounded, TN).astype(BF)
        return 0

    lax.fori_loop(0, NZ, att2, 0)
    at_in[z] = at_out[z]

    yg_out[...] = GR[1 - yh].astype(BF)
    yg = remote(yg_out, yg_in, yg_send, yg_recv, y_mate)
    yg.start()

    def at_start(r, _):
        at_copy(lax.rem(z + r, NZ)).start()
        return 0

    lax.fori_loop(1, NZ, at_start, 0)
    yg.wait_recv()
    kvg[...] = (GR[yh] + yg_in[...].astype(F32)).astype(BF)

    two, nxt, prv = lax.rem(x + 2, NX), lax.rem(x + 1, NX), lax.rem(x + 3, NX)
    order = [two, nxt, prv, x]

    def product(p, n, core):
        e = (order[n] * 2 + core) * 2 + (1 - m if p == 0 else m)
        return dot(kvg[...], W[pl.ds(pl.multiple_of(e * 512, 512), 512), :], NT)

    def cs_copy(p, n):
        return remote(cs_out.at[p, n], cs_in.at[p, n], cs_send.at[p, n], cs_recv.at[p, n], core_mate)

    def for_mate(p, n):
        cs_out[p, n] = product(p, n, 1 - c).astype(BF)
        cs_copy(p, n).start()

    def own(p, n):
        mine = product(p, n, c)
        cs_copy(p, n).wait_recv()
        R[p, n] = (mine + cs_in[p, n].astype(F32)).astype(BF)

    def by_copy(n):
        return remote(R.at[0, n, ROWS_A:256, :], by_in.at[n], by_send.at[n], by_recv.at[n], m_mate)

    def xsum(src, tmp, into, ssem, rsem):
        def at(n, half):
            return src(n, slice(half * 256, half * 256 + 256))

        firsts = [
            remote(at(0, 0), into.at[0], ssem.at[0], rsem.at[0], x_right),
            remote(at(0, 1), into.at[1], ssem.at[1], rsem.at[1], x_left),
            remote(at(1, 1), into.at[2], ssem.at[2], rsem.at[2], x_right),
            remote(at(2, 0), into.at[3], ssem.at[3], rsem.at[3], x_left),
        ]
        seconds = [
            remote(tmp.at[0], into.at[4], ssem.at[4], rsem.at[4], x_right),
            remote(tmp.at[1], into.at[5], ssem.at[5], rsem.at[5], x_left),
        ]

        def start(n):
            for i in [(0, 1), (2,), (3,), ()][n]:
                firsts[i].start()

        def relay():
            for i in range(2):
                firsts[i].wait_recv()
                tmp[i] = (at(1 + i, i)[...].astype(F32) + into[i].astype(F32)).astype(BF)
                seconds[i].start()

        def finish():
            firsts[2].wait_recv()
            firsts[3].wait_recv()
            seconds[0].wait_recv()
            seconds[1].wait_recv()
            halves = []
            for half, got in [(0, (4, 3)), (1, (2, 5))]:
                v = at(3, half)[...].astype(F32)
                for g in got:
                    v += into[g].astype(F32)
                halves.append(v)
            return halves

        def drain():
            for cp in firsts + seconds:
                cp.wait_send()

        return start, relay, finish, drain

    a0_start, a0_relay, a0_finish, a0_drain = xsum(
        lambda n, cols: R.at[0, n, 0:ROWS_A, cols],
        ax_tmp.at[0], ax_in.at[0], ax_send.at[0], ax_recv.at[0],
    )
    a1_start, a1_relay, a1_finish, a1_drain = xsum(
        lambda n, cols: R.at[1, n, 0:ROWS_A, cols],
        ax_tmp.at[1], ax_in.at[1], ax_send.at[1], ax_recv.at[1],
    )
    b_start, b_relay, b_finish, b_drain = xsum(
        lambda n, cols: RB.at[n, :, cols], bx_tmp, bx_in, bx_send, bx_recv
    )

    def add_b(n):
        by_copy(n).wait_recv()
        RB[n] = (R[1, n, ROWS_A:256, :].astype(F32) + by_in[n].astype(F32)).astype(BF)
        b_start(n)

    ay = remote(ay_out, ay_in, ay_send, ay_recv, m_mate)
    for_mate(0, 0)
    for_mate(0, 1)
    for n in range(NX):
        own(0, n)
        a0_start(n)
        by_copy(n).start()
        for_mate(*((0, n + 2) if n < 2 else (1, n - 2)))
    a0_relay()
    for n in range(NX):
        own(1, n)
        a1_start(n)
        if n < 2:
            for_mate(1, n + 2)
        add_b(n)
    fa = a0_finish()
    for half in range(2):
        ay_out[:, half * 256 : half * 256 + 256] = fa[half].astype(BF)
    ay.start()
    a1_relay()
    b_relay()

    def at_wait(r, _):
        src = lax.rem(z + NZ - r, NZ)
        remote(at_out.at[src], at_in.at[src], at_send.at[r], at_recv.at[r], at_z(src)).wait_recv()
        return 0

    lax.fori_loop(1, NZ, at_wait, 0)
    total = at_in[0].astype(F32)
    for i in range(1, NZ):
        total += at_in[i].astype(F32)
    att_ref[...] = total.T.astype(BF)

    fb = b_finish()
    for half in range(2):
        cols = slice(half * 256, half * 256 + 256)
        nbr_ref[ROWS_A:256, cols] = fb[half].astype(BF)
    fa = a1_finish()
    ay.wait_recv()
    for half in range(2):
        cols = slice(half * 256, half * 256 + 256)
        nbr_ref[0:ROWS_A, cols] = (fa[half] + ay_in[:, cols].astype(F32)).astype(BF)

    for direction in range(2):
        for u in range(4):
            for t in range(4 if u < 2 else 3):
                ag(direction, u, t).wait_send()
    for h in range(2):
        kv_copy(h).wait_send()

    def sent(r, _):
        j = lax.rem(z + r, NZ)
        info_copy(r).wait_send()
        st_copy(j).wait_send()
        res_copy(r).wait_send()
        at_copy(j).wait_send()
        return 0

    lax.fori_loop(1, NZ, sent, 0)
    yg.wait_send()

    for n in range(NX):
        for p in range(2):
            cs_copy(p, n).wait_send()
        by_copy(n).wait_send()
    ay.wait_send()
    a0_drain()
    a1_drain()
    b_drain()


def hand_over(att_from, nbr_from, att_to, nbr_to, sem):
    copies = [
        pltpu.make_async_copy(att_from, att_to, sem.at[0]),
        pltpu.make_async_copy(nbr_from, nbr_to, sem.at[1]),
    ]
    for cp in copies:
        cp.start()
    for cp in copies:
        cp.wait()


def on_device(nbr_states, kv_weight, queries, out_grad, citations):
    width = kv_weight.shape[0]
    rest = 256 - ROWS_A
    weight = kv_weight.reshape(width, 2, 2, HS).transpose(0, 2, 1, 3).reshape(width * 4, HS)
    V, D = pltpu.VMEM, pltpu.SemaphoreType.DMA
    scratch = [
        V((KC, 256, width // KC), BF),
        V((KC, width * 4 // KC, HS), BF),
        V((width, 512), BF),
        V((256, 256), F32),
        V((NZ, 2, 256, 256), BF),
        V((2, 2, 256, 256), BF),
        V((NZ, 8, 256), F32),
        V((NZ, 8, 256), F32),
        V((NZ, 2, 256, 256), F32),
        V((NZ, 2, 256, 256), F32),
        V((NZ, 8, 256), F32),
        V((NZ, 8, 256), F32),
        V((8, 256), F32),
        V((NZ, 8, 256), F32),
        V((NZ, 256, 256), BF),
        V((NZ, 256, 256), BF),
        V((2, 256, 512), F32),
        V((256, 512), BF),
        V((256, 512), BF),
        V((256, 512), BF),
        V((2, NX, 256, 512), BF),
        V((2, NX, 256, 512), BF),
        V((2, NX, 256, 512), BF),
        V((NX, rest, 512), BF),
        V((NX, rest, 512), BF),
        V((2, 6, ROWS_A, 256), BF),
        V((2, 2, ROWS_A, 256), BF),
        V((6, rest, 256), BF),
        V((2, rest, 256), BF),
        V((ROWS_A, 512), BF),
        V((ROWS_A, 512), BF),
        V((256, 256), BF),
        D((2, KC)),
        D((2,)),
        D((2, 4, 4)), D((2, 4, 4)),
        D((2,)), D((2,)),
        D((NZ,)), D((NZ,)),
        D((NZ,)), D((NZ,)),
        D((NZ,)), D((NZ,)),
        D((NZ,)), D((NZ,)),
        D, D,
        D((2, NX)), D((2, NX)),
        D((NX,)), D((NX,)),
        D((2, 6)), D((2, 6)),
        D((6,)), D((6,)),
        D, D,
    ]
    vmem = pl.BlockSpec(memory_space=pltpu.VMEM)
    hbm = pl.BlockSpec(memory_space=pl.ANY)
    shapes = (jax.ShapeDtypeStruct((256, 256), BF), jax.ShapeDtypeStruct((256, 512), BF))
    results = pl.pallas_call(
        kernel,
        out_shape=shapes,
        in_specs=[pl.BlockSpec(memory_space=pltpu.SMEM), hbm, hbm, hbm, hbm],
        out_specs=(vmem, vmem),
        scratch_shapes=scratch,
        compiler_params=pltpu.CompilerParams(
            collective_id=0, has_side_effects=True, vmem_limit_bytes=56 * 2**20
        ),
        cost_estimate=pl.CostEstimate(
            flops=6 * 10**9, bytes_accessed=13 * 2**20, transcendentals=2 * 10**6
        ),
    )(citations.T, queries, out_grad, nbr_states, weight)
    return pl.pallas_call(
        hand_over,
        out_shape=shapes,
        in_specs=[hbm, hbm],
        out_specs=(hbm, hbm),
        scratch_shapes=[D((2,))],
    )(*results)


def solution(mesh):
    heads = ("section", "mp")
    return jax.shard_map(
        on_device,
        mesh=mesh,
        in_specs=(
            P("dp", None),
            P(None, None, heads),
            P("dp", heads),
            P("dp", heads),
            P("dp", None),
        ),
        out_specs=(P("dp", heads), P("dp", heads)),
        check_vma=False,
    )
```

```python
import functools

import jax
import jax.numpy as jnp
from jax import lax
from jax.experimental import pallas as pl
from jax.experimental.pallas import tpu as pltpu
from jax.sharding import PartitionSpec as P

HS = 128
CH = 64
CL = 128
NZ = 8
NX = 4
KC = 8
ROWS_A = 144
NEG = -1e30
BF = jnp.bfloat16
F32 = jnp.float32
NT = (((1,), (1,)), ((), ()))
NN = (((1,), (0,)), ((), ()))
TN = (((0,), (0,)), ((), ()))


def dot(a, b, dims):
    return lax.dot_general(a, b, dims, preferred_element_type=F32)


def kernel(
    cit_ref, q_hbm, g_hbm, x_hbm, w_hbm, att_ref, nbr_ref,
    X, W32, W, acc, G, KV, info_out, info_in, E, DP, st_out, st_in, res_out, res_in,
    at_out, at_in, GR, yg_out, yg_in, kvg, cs_out, cs_in, R, by_in, RB,
    ax_in, ax_tmp, bx_in, bx_tmp, ay_out, ay_in, PM, PRE,
    ld_sem, own_sem, ag_send, ag_recv, kv_send, kv_recv, inf_send, inf_recv, st_send, st_recv,
    rs_send, rs_recv, at_send, at_recv, yg_send, yg_recv, cs_send, cs_recv,
    by_send, by_recv, ax_send, ax_recv, bx_send, bx_recv, ay_send, ay_recv,
):
    s, d, m = lax.axis_index("section"), lax.axis_index("dp"), lax.axis_index("mp")
    x, c = s // 2, s % 2
    yh, z = d // NZ, d % NZ
    depth = x_hbm.shape[1] // KC
    scaling = 1.0 / HS**0.5

    def at_z(zt):
        return {"dp": yh * NZ + zt}

    y_mate = {"dp": (1 - yh) * NZ + z}
    core_mate = {"section": x * 2 + (1 - c)}
    x_right = {"section": lax.rem(x + 1, NX) * 2 + c}
    x_left = {"section": lax.rem(x + NX - 1, NX) * 2 + c}
    m_mate = {"mp": 1 - m}

    def remote(src, dst, ssem, rsem, dev):
        return pltpu.make_async_remote_copy(
            src_ref=src, dst_ref=dst, send_sem=ssem, recv_sem=rsem,
            device_id=dev, device_id_type=pl.DeviceIdType.MESH,
        )

    def x_load(k):
        return pltpu.make_async_copy(
            x_hbm.at[:, pl.ds(pl.multiple_of(k * depth, depth), depth)], X.at[k], ld_sem.at[1, k]
        )

    def w_load(k):
        return pltpu.make_async_copy(
            w_hbm.at[pl.ds(pl.multiple_of(k * 4 * depth, depth), 4 * depth), :], W32.at[k], ld_sem.at[0, k]
        )

    own_rows = [pltpu.make_async_copy(src, G.at[z, i], own_sem.at[i]) for i, src in enumerate([q_hbm, g_hbm])]
    for cp in own_rows:
        cp.start()

    def start_loads(k, _):
        w_load(k).start()
        x_load(k).start()
        return 0

    lax.fori_loop(0, KC, start_loads, 0)

    barrier = pltpu.get_barrier_semaphore()
    for dev in [at_z(lax.rem(z + r, NZ)) for r in range(1, NZ)] + [
        y_mate, core_mate, x_right, x_left, m_mate
    ]:
        pl.semaphore_signal(barrier, inc=1, device_id=dev, device_id_type=pl.DeviceIdType.MESH)

    lane = lax.broadcasted_iota(jnp.int32, (16, 256), 1) // CH
    owner = lax.broadcasted_iota(jnp.int32, (16, 256), 0)
    ids = []
    for k in range(2):
        v = jnp.zeros((16, 256), jnp.int32)
        for b in range(4):
            v = jnp.where(lane == b, cit_ref[k, b], v)
        ids.append(v)
    second = (ids[0] == owner * 2 + 1) | (ids[1] == owner * 2 + 1)
    first = (ids[0] == owner * 2) | (ids[1] == owner * 2)
    cited = jnp.where(first | second, 1.0, 0.0).astype(F32)
    sel = jnp.where(second, 1.0, 0.0).astype(F32)
    sel = jnp.max(sel, axis=1, keepdims=True) + jnp.zeros((16, 256), F32)
    for t in range(NZ):
        for w in range(2):
            o = w * NZ + t
            info_out[t, w : w + 1, :] = cited[o : o + 1]
            info_out[t, 2 + w : 3 + w, :] = sel[o : o + 1]
        info_out[t, 4:8, :] = jnp.zeros((4, 256), F32)
    info_in[z] = info_out[z]
    for cp in own_rows:
        cp.wait()
    pl.semaphore_wait(barrier, 12)

    def ag(direction, u, t):
        if direction == 0:
            home, to, arr = lax.rem(z - t + NZ, NZ), lax.rem(z + 1, NZ), u // 2
        else:
            home, to, arr = lax.rem(z + t, NZ), lax.rem(z + NZ - 1, NZ), 1 - u // 2
        piece = G.at[home, arr, pl.ds(pl.multiple_of((u % 2) * 128, 128), 128)]
        return remote(piece, piece, ag_send.at[direction, u, t], ag_recv.at[direction, u, t], at_z(to))

    for u in range(4):
        for direction in range(2):
            ag(direction, u, 0).start()

    def info_copy(r):
        to = lax.rem(z + r, NZ)
        return remote(info_out.at[to], info_in.at[z], inf_send.at[r], inf_recv.at[r], at_z(to))

    def info_start(r, _):
        info_copy(r).start()
        return 0

    lax.fori_loop(1, NZ, info_start, 0)

    def relay(t, u):
        for direction in range(2):
            ag(direction, u, t - 1).wait_recv()
            ag(direction, u, t).start()

    def arrived(t, u):
        for direction in range(2):
            ag(direction, u, t).wait_recv()

    out_row = lax.broadcasted_iota(jnp.int32, (256, 256), 0)
    in_row = lax.broadcasted_iota(jnp.int32, (256, 256), 1)
    PM[...] = jnp.where(in_row == (out_row % 64) * 4 + out_row // 64, 1.0, 0.0).astype(BF)

    def piece(k, _):
        w_load(k).wait()

        def sort(i, _):
            for u in range(4):
                b = i * 4 + u
                got = dot(PM[...], W32[k, pl.ds(pl.multiple_of(b * 256, 256), 256), :], NN).astype(BF)
                rows = pl.ds(pl.multiple_of(k * depth + b * 64, 64), 64)
                for n in range(4):
                    W[rows, n * HS : n * HS + HS] = got[n * 64 : n * 64 + 64]
            return 0

        lax.fori_loop(0, depth // 256, sort, 0)
        x_load(k).wait()
        rows = pl.ds(pl.multiple_of(k * depth, depth), depth)
        acc[...] += dot(X[k], W[rows, 0:256], NN)

        @pl.when(k >= 2)
        def _():
            relay(1 + (k - 2) // 4, (k - 2) % 4)

        return 0

    def piece_1(k, _):
        rows = pl.ds(pl.multiple_of(k * depth, depth), depth)
        acc[...] += dot(X[k], W[rows, 256:512], NN)
        return 0

    def kv_copy(h):
        return remote(KV.at[yh, h], KV.at[yh, h], kv_send.at[h], kv_recv.at[h], y_mate)

    for h, body in enumerate([piece, piece_1]):
        acc[...] = jnp.zeros_like(acc)
        lax.fori_loop(0, KC, body, 0)
        KV[yh, h] = acc[...].astype(BF)
        kv_copy(h).start()

    def kv_wait(h):
        pltpu.make_async_remote_copy(
            src_ref=KV.at[1 - yh, h], dst_ref=KV.at[1 - yh, h], send_sem=kv_send.at[h],
            recv_sem=kv_recv.at[h], device_id=y_mate, device_id_type=pl.DeviceIdType.MESH,
        ).wait_recv()

    def info_wait(r, _):
        info_copy(r).wait_recv()
        return 0

    relay(2, 2)
    relay(2, 3)
    lax.fori_loop(1, NZ, info_wait, 0)
    relay(3, 0)
    relay(3, 1)
    for h in range(2):
        kv_wait(h)

    def chosen(j, h):
        out = []
        for w in range(2):
            f = info_in[j, 2 + w : 3 + w, :] + jnp.zeros((CL, 256), F32)
            one, zero = f.astype(BF), (1.0 - f).astype(BF)
            out.append(KV[w, h, 0:CL, :] * zero + KV[w, h, CL : 2 * CL, :] * one)
        return jnp.concatenate(out, axis=0)

    def st_copy(j):
        r = lax.rem(j - z + NZ, NZ)
        return remote(st_out.at[j], st_in.at[z], st_send.at[r], st_recv.at[r], at_z(j))

    def att1(j):
        for h in range(2):
            kv = chosen(j, h)
            cols = slice(h * HS, h * HS + HS)
            sc = dot(kv[:, :HS], G[j, 0, :, cols], NT) * scaling
            sc = jnp.concatenate(
                [
                    jnp.where(info_in[j, w : w + 1, :] > 0.0, sc[w * CL : w * CL + CL], NEG)
                    for w in range(2)
                ],
                axis=0,
            )
            top = jnp.max(sc, axis=0, keepdims=True)
            e = jnp.exp(sc - top)
            dp = dot(kv[:, HS:], G[j, 1, :, cols], NT)
            E[j, h] = e
            DP[j, h] = dp
            st_out[j, 3 * h : 3 * h + 1, :] = top
            st_out[j, 3 * h + 1 : 3 * h + 2, :] = jnp.sum(e, axis=0, keepdims=True)
            st_out[j, 3 * h + 2 : 3 * h + 3, :] = jnp.sum(e * dp, axis=0, keepdims=True)
        st_out[j, 6:8, :] = jnp.zeros((2, 256), F32)

    def both(t):
        def side(i, _):
            j = lax.rem(z + NZ - t + 2 * i * t, NZ)
            att1(j)
            st_copy(j).start()
            return 0

        lax.fori_loop(0, 1 if t == 4 else 2, side, 0)

    att1(z)
    both(1)
    both(2)
    arrived(2, 2)
    arrived(2, 3)
    both(3)
    arrived(3, 0)
    arrived(3, 1)
    both(4)

    st_in[z] = st_out[z]

    def st_wait(r, _):
        src = lax.rem(z + NZ - r, NZ)
        remote(st_out.at[src], st_in.at[src], st_send.at[r], st_recv.at[r], at_z(src)).wait_recv()
        return 0

    lax.fori_loop(1, NZ, st_wait, 0)
    for h in range(2):
        tops = [st_in[i, 3 * h : 3 * h + 1, :] for i in range(NZ)]
        top = functools.reduce(jnp.maximum, tops)
        total = jnp.zeros((1, 256), F32)
        dots = jnp.zeros((1, 256), F32)
        for i in range(NZ):
            f = jnp.exp(tops[i] - top)
            total += f * st_in[i, 3 * h + 1 : 3 * h + 2, :]
            dots += f * st_in[i, 3 * h + 2 : 3 * h + 3, :]
        res_out[3 * h : 3 * h + 1, :] = top
        res_out[3 * h + 1 : 3 * h + 2, :] = 1.0 / total
        res_out[3 * h + 2 : 3 * h + 3, :] = dots / total
    res_out[6:8, :] = jnp.zeros((2, 256), F32)
    res_in[z] = res_out[...]

    def res_copy(r):
        return remote(res_out, res_in.at[z], rs_send.at[r], rs_recv.at[r], at_z(lax.rem(z + r, NZ)))

    for r in (4, 5, 3, 6, 2, 7, 1):
        res_copy(r).start()
    GR[...] = jnp.zeros_like(GR)

    def at_copy(j):
        r = lax.rem(j - z + NZ, NZ)
        return remote(at_out.at[j], at_in.at[z], at_send.at[r], at_recv.at[r], at_z(j))

    def yg_copy(h):
        return remote(yg_out.at[h], yg_in.at[h], yg_send.at[h], yg_recv.at[h], y_mate)

    for h in range(2):
        cols = slice(h * HS, h * HS + HS)
        wide = slice(h * 256, h * 256 + 256)

        def att2(r, _):
            j = lax.rem(z + NZ - r, NZ)
            if h == 0:

                @pl.when(r > 0)
                def _():
                    remote(res_out, res_in.at[j], rs_send.at[r], rs_recv.at[r], at_z(j)).wait_recv()

            f = jnp.exp(st_out[j, 3 * h : 3 * h + 1, :] - res_in[j, 3 * h : 3 * h + 1, :])
            p = E[j, h] * (f * res_in[j, 3 * h + 1 : 3 * h + 2, :])
            rounded = p.astype(BF)
            ds = (p * (DP[j, h] - res_in[j, 3 * h + 2 : 3 * h + 3, :])).astype(BF)
            kg = dot(ds, G[j, 0, :, cols], NN) * scaling
            vg = dot(rounded, G[j, 1, :, cols], NN)
            part = jnp.concatenate([kg, vg], axis=1)
            for w in range(2):
                one = info_in[j, 2 + w : 3 + w, :]
                mine = part[w * CL : w * CL + CL]
                GR[w, 0:CL, wide] += mine * (1.0 - one)
                GR[w, CL : 2 * CL, wide] += mine * one
            values = chosen(j, h)[:, HS:]
            at_out[j, cols, :] = dot(values, rounded, TN).astype(BF)
            return 0

        lax.fori_loop(0, NZ, att2, 0)
        yg_out[h] = GR[1 - yh, :, wide].astype(BF)
        yg_copy(h).start()

    def at_start(r, _):
        at_copy(lax.rem(z + r, NZ)).start()
        return 0

    lax.fori_loop(1, NZ, at_start, 0)
    at_in[z] = at_out[z]

    def add_mate(h):
        wide = slice(h * 256, h * 256 + 256)
        yg_copy(h).wait_recv()
        kvg[:, wide] = (GR[yh, :, wide] + yg_in[h].astype(F32)).astype(BF)

    add_mate(0)

    two, nxt, prv = lax.rem(x + 2, NX), lax.rem(x + 1, NX), lax.rem(x + 3, NX)
    order = [two, nxt, prv, x]

    def w_rows(p, n, core):
        e = (order[n] * 2 + core) * 2 + (1 - m if p == 0 else m)
        return pl.ds(pl.multiple_of(e * 512, 512), 512)

    def half(p, n, core, h):
        wide = slice(h * 256, h * 256 + 256)
        return dot(kvg[:, wide], W[w_rows(p, n, core), wide], NT)

    early = {(0, 0, 0): 0, (0, 1, 0): 1, (0, 0, 1): 2}
    for (p, n, mine), i in early.items():
        PRE[i] = half(p, n, c if mine else 1 - c, 0)
    add_mate(1)

    def product(p, n, mine):
        core = c if mine else 1 - c
        if (p, n, mine) in early:
            return PRE[early[p, n, mine]] + half(p, n, core, 1)
        return dot(kvg[...], W[w_rows(p, n, core), :], NT)

    def cs_copy(p, n):
        return remote(cs_out.at[p, n], cs_in.at[p, n], cs_send.at[p, n], cs_recv.at[p, n], core_mate)

    def for_mate(p, n):
        cs_out[p, n] = product(p, n, 0).astype(BF)
        cs_copy(p, n).start()

    def own(p, n):
        mine = product(p, n, 1)
        cs_copy(p, n).wait_recv()
        R[p, n] = (mine + cs_in[p, n].astype(F32)).astype(BF)

    def by_copy(n):
        return remote(R.at[0, n, ROWS_A:256, :], by_in.at[n], by_send.at[n], by_recv.at[n], m_mate)

    def xsum(src, tmp, into, ssem, rsem):
        def at(n, half):
            return src(n, slice(half * 256, half * 256 + 256))

        firsts = [
            remote(at(0, 0), into.at[0], ssem.at[0], rsem.at[0], x_right),
            remote(at(0, 1), into.at[1], ssem.at[1], rsem.at[1], x_left),
            remote(at(1, 1), into.at[2], ssem.at[2], rsem.at[2], x_right),
            remote(at(2, 0), into.at[3], ssem.at[3], rsem.at[3], x_left),
        ]
        seconds = [
            remote(tmp.at[0], into.at[4], ssem.at[4], rsem.at[4], x_right),
            remote(tmp.at[1], into.at[5], ssem.at[5], rsem.at[5], x_left),
        ]

        def start(n):
            for i in [(0, 1), (2,), (3,), ()][n]:
                firsts[i].start()

        def relay():
            for i in range(2):
                firsts[i].wait_recv()
                tmp[i] = (at(1 + i, i)[...].astype(F32) + into[i].astype(F32)).astype(BF)
                seconds[i].start()

        def finish():
            firsts[2].wait_recv()
            firsts[3].wait_recv()
            seconds[0].wait_recv()
            seconds[1].wait_recv()
            halves = []
            for half, got in [(0, (4, 3)), (1, (2, 5))]:
                v = at(3, half)[...].astype(F32)
                for g in got:
                    v += into[g].astype(F32)
                halves.append(v)
            return halves

        def drain():
            for cp in firsts + seconds:
                cp.wait_send()

        return start, relay, finish, drain

    a0_start, a0_relay, a0_finish, a0_drain = xsum(
        lambda n, cols: R.at[0, n, 0:ROWS_A, cols],
        ax_tmp.at[0], ax_in.at[0], ax_send.at[0], ax_recv.at[0],
    )
    a1_start, a1_relay, a1_finish, a1_drain = xsum(
        lambda n, cols: R.at[1, n, 0:ROWS_A, cols],
        ax_tmp.at[1], ax_in.at[1], ax_send.at[1], ax_recv.at[1],
    )
    b_start, b_relay, b_finish, b_drain = xsum(
        lambda n, cols: RB.at[n, :, cols], bx_tmp, bx_in, bx_send, bx_recv
    )

    def add_b(n):
        by_copy(n).wait_recv()
        RB[n] = (R[1, n, ROWS_A:256, :].astype(F32) + by_in[n].astype(F32)).astype(BF)
        b_start(n)

    ay = remote(ay_out, ay_in, ay_send, ay_recv, m_mate)
    for_mate(0, 0)
    for_mate(0, 1)
    for n in range(NX):
        own(0, n)
        a0_start(n)
        by_copy(n).start()
        for_mate(*((0, n + 2) if n < 2 else (1, n - 2)))
    a0_relay()
    for n in range(NX):
        own(1, n)
        a1_start(n)
        if n < 2:
            for_mate(1, n + 2)
    add_b(0)
    fa = a0_finish()
    for half_ in range(2):
        ay_out[:, half_ * 256 : half_ * 256 + 256] = fa[half_].astype(BF)
    ay.start()
    a1_relay()
    add_b(1)
    add_b(2)
    b_relay()
    add_b(3)

    def at_wait(r, _):
        src = lax.rem(z + NZ - r, NZ)
        remote(at_out.at[src], at_in.at[src], at_send.at[r], at_recv.at[r], at_z(src)).wait_recv()
        return 0

    lax.fori_loop(1, NZ, at_wait, 0)
    total = at_in[0].astype(F32)
    for i in range(1, NZ):
        total += at_in[i].astype(F32)
    att_ref[...] = total.T.astype(BF)

    fb = b_finish()
    for half in range(2):
        cols = slice(half * 256, half * 256 + 256)
        nbr_ref[ROWS_A:256, cols] = fb[half].astype(BF)
    fa = a1_finish()
    ay.wait_recv()
    for half in range(2):
        cols = slice(half * 256, half * 256 + 256)
        nbr_ref[0:ROWS_A, cols] = (fa[half] + ay_in[:, cols].astype(F32)).astype(BF)

    for direction in range(2):
        for u in range(4):
            for t in range(4 if u < 2 else 3):
                ag(direction, u, t).wait_send()
    for h in range(2):
        kv_copy(h).wait_send()

    def sent(r, _):
        j = lax.rem(z + r, NZ)
        info_copy(r).wait_send()
        st_copy(j).wait_send()
        res_copy(r).wait_send()
        at_copy(j).wait_send()
        return 0

    lax.fori_loop(1, NZ, sent, 0)
    for h in range(2):
        yg_copy(h).wait_send()

    for n in range(NX):
        for p in range(2):
            cs_copy(p, n).wait_send()
        by_copy(n).wait_send()
    ay.wait_send()
    a0_drain()
    a1_drain()
    b_drain()


def hand_over(att_from, nbr_from, att_to, nbr_to):
    att_to[...] = att_from[...]
    nbr_to[...] = nbr_from[...]


def on_device(nbr_states, kv_weight, queries, out_grad, citations):
    width = kv_weight.shape[0]
    rest = 256 - ROWS_A
    weight = kv_weight.reshape(width, 2, 2, HS).transpose(0, 2, 1, 3).reshape(width * 4, HS)
    V, D = pltpu.VMEM, pltpu.SemaphoreType.DMA
    scratch = [
        V((KC, 256, width // KC), BF),
        V((KC, width * 4 // KC, HS), BF),
        V((width, 512), BF),
        V((256, 256), F32),
        V((NZ, 2, 256, 256), BF),
        V((2, 2, 256, 256), BF),
        V((NZ, 8, 256), F32),
        V((NZ, 8, 256), F32),
        V((NZ, 2, 256, 256), F32),
        V((NZ, 2, 256, 256), F32),
        V((NZ, 8, 256), F32),
        V((NZ, 8, 256), F32),
        V((8, 256), F32),
        V((NZ, 8, 256), F32),
        V((NZ, 256, 256), BF),
        V((NZ, 256, 256), BF),
        V((2, 256, 512), F32),
        V((2, 256, 256), BF),
        V((2, 256, 256), BF),
        V((256, 512), BF),
        V((2, NX, 256, 512), BF),
        V((2, NX, 256, 512), BF),
        V((2, NX, 256, 512), BF),
        V((NX, rest, 512), BF),
        V((NX, rest, 512), BF),
        V((2, 6, ROWS_A, 256), BF),
        V((2, 2, ROWS_A, 256), BF),
        V((6, rest, 256), BF),
        V((2, rest, 256), BF),
        V((ROWS_A, 512), BF),
        V((ROWS_A, 512), BF),
        V((256, 256), BF),
        V((3, 256, 512), F32),
        D((2, KC)),
        D((2,)),
        D((2, 4, 4)), D((2, 4, 4)),
        D((2,)), D((2,)),
        D((NZ,)), D((NZ,)),
        D((NZ,)), D((NZ,)),
        D((NZ,)), D((NZ,)),
        D((NZ,)), D((NZ,)),
        D((2,)), D((2,)),
        D((2, NX)), D((2, NX)),
        D((NX,)), D((NX,)),
        D((2, 6)), D((2, 6)),
        D((6,)), D((6,)),
        D, D,
    ]
    vmem = pl.BlockSpec(memory_space=pltpu.VMEM)
    hbm = pl.BlockSpec(memory_space=pl.ANY)
    shapes = (jax.ShapeDtypeStruct((256, 256), BF), jax.ShapeDtypeStruct((256, 512), BF))
    results = pl.pallas_call(
        kernel,
        out_shape=shapes,
        in_specs=[pl.BlockSpec(memory_space=pltpu.SMEM), hbm, hbm, hbm, hbm],
        out_specs=(vmem, vmem),
        scratch_shapes=scratch,
        compiler_params=pltpu.CompilerParams(
            collective_id=0, has_side_effects=True, vmem_limit_bytes=56 * 2**20
        ),
        cost_estimate=pl.CostEstimate(
            flops=6 * 10**9, bytes_accessed=13 * 2**20, transcendentals=2 * 10**6
        ),
    )(citations.T, queries, out_grad, nbr_states, weight)
    return pl.pallas_call(
        hand_over,
        out_shape=shapes,
        in_specs=[vmem, vmem],
        out_specs=(vmem, vmem),
    )(*results)


def solution(mesh):
    heads = ("section", "mp")
    return jax.shard_map(
        on_device,
        mesh=mesh,
        in_specs=(
            P("dp", None),
            P(None, None, heads),
            P("dp", heads),
            P("dp", heads),
            P("dp", None),
        ),
        out_specs=(P("dp", heads), P("dp", heads)),
        check_vma=False,
    )
```

```python
import functools

import jax
import jax.numpy as jnp
from jax import lax
from jax.experimental import pallas as pl
from jax.experimental.pallas import tpu as pltpu
from jax.sharding import PartitionSpec as P

HS = 128
CH = 64
CL = 128
NZ = 8
NX = 4
KC = 8
ROWS_A = 144
NEG = -1e30
BF = jnp.bfloat16
F32 = jnp.float32
NT = (((1,), (1,)), ((), ()))
NN = (((1,), (0,)), ((), ()))
TN = (((0,), (0,)), ((), ()))


def dot(a, b, dims):
    return lax.dot_general(a, b, dims, preferred_element_type=F32)


def kernel(
    cit_ref, q_hbm, g_hbm, x_hbm, w_hbm, att_ref, nbr_ref,
    X, W32, W, acc, G, KV, info_out, info_in, E, DP, st_out, st_in, res_out, res_in,
    far_in, at_out, at_in, GR, yg_out, yg_in, kvg, cs_out, cs_in, R, by_in, RB,
    ax_in, ax_tmp, bx_in, bx_tmp, ay_out, ay_in, PM, PRE,
    ld_sem, own_sem, ag_send, ag_recv, kv_send, kv_recv, inf_send, inf_recv, st_send, st_recv,
    rs_send, rs_recv, far_send, far_recv, at_send, at_recv, yg_send, yg_recv, cs_send, cs_recv,
    by_send, by_recv, ax_send, ax_recv, bx_send, bx_recv, ay_send, ay_recv,
):
    s, d, m = lax.axis_index("section"), lax.axis_index("dp"), lax.axis_index("mp")
    x, c = s // 2, s % 2
    yh, z = d // NZ, d % NZ
    depth = x_hbm.shape[1] // KC
    scaling = 1.0 / HS**0.5

    def at_z(zt):
        return {"dp": yh * NZ + zt}

    y_mate = {"dp": (1 - yh) * NZ + z}
    core_mate = {"section": x * 2 + (1 - c)}
    x_right = {"section": lax.rem(x + 1, NX) * 2 + c}
    x_left = {"section": lax.rem(x + NX - 1, NX) * 2 + c}
    m_mate = {"mp": 1 - m}

    def remote(src, dst, ssem, rsem, dev):
        return pltpu.make_async_remote_copy(
            src_ref=src, dst_ref=dst, send_sem=ssem, recv_sem=rsem,
            device_id=dev, device_id_type=pl.DeviceIdType.MESH,
        )

    def x_load(k):
        return pltpu.make_async_copy(
            x_hbm.at[:, pl.ds(pl.multiple_of(k * depth, depth), depth)], X.at[k], ld_sem.at[1, k]
        )

    def w_load(k):
        return pltpu.make_async_copy(
            w_hbm.at[pl.ds(pl.multiple_of(k * 4 * depth, depth), 4 * depth), :], W32.at[k], ld_sem.at[0, k]
        )

    own_rows = [pltpu.make_async_copy(src, G.at[z, i], own_sem.at[i]) for i, src in enumerate([q_hbm, g_hbm])]
    for cp in own_rows:
        cp.start()

    def start_loads(k, _):
        w_load(k).start()
        x_load(k).start()
        return 0

    lax.fori_loop(0, KC, start_loads, 0)

    barrier = pltpu.get_barrier_semaphore()
    for dev in [at_z(lax.rem(z + r, NZ)) for r in range(1, NZ)] + [
        y_mate, core_mate, x_right, x_left, m_mate
    ]:
        pl.semaphore_signal(barrier, inc=1, device_id=dev, device_id_type=pl.DeviceIdType.MESH)

    lane = lax.broadcasted_iota(jnp.int32, (16, 256), 1) // CH
    owner = lax.broadcasted_iota(jnp.int32, (16, 256), 0)
    ids = []
    for k in range(2):
        v = jnp.zeros((16, 256), jnp.int32)
        for b in range(4):
            v = jnp.where(lane == b, cit_ref[k, b], v)
        ids.append(v)
    second = (ids[0] == owner * 2 + 1) | (ids[1] == owner * 2 + 1)
    first = (ids[0] == owner * 2) | (ids[1] == owner * 2)
    cited = jnp.where(first | second, 1.0, 0.0).astype(F32)
    sel = jnp.where(second, 1.0, 0.0).astype(F32)
    sel = jnp.max(sel, axis=1, keepdims=True) + jnp.zeros((16, 256), F32)
    for t in range(NZ):
        for w in range(2):
            o = w * NZ + t
            info_out[t, w : w + 1, :] = cited[o : o + 1]
            info_out[t, 2 + w : 3 + w, :] = sel[o : o + 1]
        info_out[t, 4:8, :] = jnp.zeros((4, 256), F32)
    info_in[z] = info_out[z]
    for cp in own_rows:
        cp.wait()
    pl.semaphore_wait(barrier, 12)

    def ag(direction, u, t):
        if direction == 0:
            home, to, arr = lax.rem(z - t + NZ, NZ), lax.rem(z + 1, NZ), u // 2
        else:
            home, to, arr = lax.rem(z + t, NZ), lax.rem(z + NZ - 1, NZ), 1 - u // 2
        piece = G.at[home, arr, pl.ds(pl.multiple_of((u % 2) * 128, 128), 128)]
        return remote(piece, piece, ag_send.at[direction, u, t], ag_recv.at[direction, u, t], at_z(to))

    for u in range(4):
        for direction in range(2):
            ag(direction, u, 0).start()

    def info_copy(r):
        to = lax.rem(z + r, NZ)
        return remote(info_out.at[to], info_in.at[z], inf_send.at[r], inf_recv.at[r], at_z(to))

    def info_start(r, _):
        info_copy(r).start()
        return 0

    lax.fori_loop(1, NZ, info_start, 0)

    def relay(t, u):
        for direction in range(2):
            ag(direction, u, t - 1).wait_recv()
            ag(direction, u, t).start()

    def arrived(t, u):
        for direction in range(2):
            ag(direction, u, t).wait_recv()

    out_row = lax.broadcasted_iota(jnp.int32, (256, 256), 0)
    in_row = lax.broadcasted_iota(jnp.int32, (256, 256), 1)
    PM[...] = jnp.where(in_row == (out_row % 64) * 4 + out_row // 64, 1.0, 0.0).astype(BF)

    def piece(k, _):
        w_load(k).wait()

        def sort(i, _):
            for u in range(4):
                b = i * 4 + u
                got = dot(PM[...], W32[k, pl.ds(pl.multiple_of(b * 256, 256), 256), :], NN).astype(BF)
                rows = pl.ds(pl.multiple_of(k * depth + b * 64, 64), 64)
                for n in range(4):
                    W[rows, n * HS : n * HS + HS] = got[n * 64 : n * 64 + 64]
            return 0

        lax.fori_loop(0, depth // 256, sort, 0)
        x_load(k).wait()
        rows = pl.ds(pl.multiple_of(k * depth, depth), depth)
        acc[...] += dot(X[k], W[rows, 0:256], NN)

        @pl.when(k >= 2)
        def _():
            relay(1 + (k - 2) // 4, (k - 2) % 4)

        return 0

    def piece_1(k, _):
        rows = pl.ds(pl.multiple_of(k * depth, depth), depth)
        acc[...] += dot(X[k], W[rows, 256:512], NN)
        return 0

    def kv_copy(h):
        return remote(KV.at[yh, h], KV.at[yh, h], kv_send.at[h], kv_recv.at[h], y_mate)

    for h, body in enumerate([piece, piece_1]):
        acc[...] = jnp.zeros_like(acc)
        lax.fori_loop(0, KC, body, 0)
        KV[yh, h] = acc[...].astype(BF)
        kv_copy(h).start()

    def kv_wait(h):
        pltpu.make_async_remote_copy(
            src_ref=KV.at[1 - yh, h], dst_ref=KV.at[1 - yh, h], send_sem=kv_send.at[h],
            recv_sem=kv_recv.at[h], device_id=y_mate, device_id_type=pl.DeviceIdType.MESH,
        ).wait_recv()

    def info_wait(r, _):
        info_copy(r).wait_recv()
        return 0

    relay(2, 2)
    relay(2, 3)
    lax.fori_loop(1, NZ, info_wait, 0)
    relay(3, 0)
    relay(3, 1)
    for h in range(2):
        kv_wait(h)

    def chosen(j, h):
        out = []
        for w in range(2):
            f = info_in[j, 2 + w : 3 + w, :] + jnp.zeros((CL, 256), F32)
            one, zero = f.astype(BF), (1.0 - f).astype(BF)
            out.append(KV[w, h, 0:CL, :] * zero + KV[w, h, CL : 2 * CL, :] * one)
        return jnp.concatenate(out, axis=0)

    def st_copy(j):
        r = lax.rem(j - z + NZ, NZ)
        return remote(st_out.at[j], st_in.at[z], st_send.at[r], st_recv.at[r], at_z(j))

    def att1(j):
        for h in range(2):
            kv = chosen(j, h)
            cols = slice(h * HS, h * HS + HS)
            sc = dot(kv[:, :HS], G[j, 0, :, cols], NT) * scaling
            sc = jnp.concatenate(
                [
                    jnp.where(info_in[j, w : w + 1, :] > 0.0, sc[w * CL : w * CL + CL], NEG)
                    for w in range(2)
                ],
                axis=0,
            )
            top = jnp.max(sc, axis=0, keepdims=True)
            e = jnp.exp(sc - top)
            dp = dot(kv[:, HS:], G[j, 1, :, cols], NT)
            E[j, h] = e
            DP[j, h] = dp
            st_out[j, 3 * h : 3 * h + 1, :] = top
            st_out[j, 3 * h + 1 : 3 * h + 2, :] = jnp.sum(e, axis=0, keepdims=True)
            st_out[j, 3 * h + 2 : 3 * h + 3, :] = jnp.sum(e * dp, axis=0, keepdims=True)
        st_out[j, 6:8, :] = jnp.zeros((2, 256), F32)

    def both(t):
        def side(i, _):
            j = lax.rem(z + NZ - t + 2 * i * t, NZ)
            att1(j)
            st_copy(j).start()
            return 0

        lax.fori_loop(0, 2, side, 0)

    far = lax.rem(z + 4, NZ)

    def far_copy(r):
        return remote(st_out.at[far], far_in.at[far], far_send.at[r], far_recv.at[r], at_z(lax.rem(z + r, NZ)))

    both(1)
    both(2)
    arrived(2, 2)
    arrived(2, 3)
    both(3)
    att1(z)
    arrived(3, 0)
    arrived(3, 1)
    att1(far)
    far_in[far] = st_out[far]
    for r in (4, 5, 3, 6, 2, 7, 1):
        far_copy(r).start()

    near = (0, 1, 2, 3, 5, 6, 7)
    st_in[z] = st_out[z]
    for r in near[1:]:
        src = lax.rem(z + NZ - r, NZ)
        remote(st_out.at[src], st_in.at[src], st_send.at[r], st_recv.at[r], at_z(src)).wait_recv()
    for h in range(2):
        stats = [[st_in[lax.rem(z + NZ - r, NZ), 3 * h + i : 3 * h + i + 1, :] for i in range(3)] for r in near]
        top = functools.reduce(jnp.maximum, [v[0] for v in stats])
        total = jnp.zeros((1, 256), F32)
        dots = jnp.zeros((1, 256), F32)
        for v in stats:
            f = jnp.exp(v[0] - top)
            total += f * v[1]
            dots += f * v[2]
        res_out[3 * h : 3 * h + 1, :] = top
        res_out[3 * h + 1 : 3 * h + 2, :] = total
        res_out[3 * h + 2 : 3 * h + 3, :] = dots
    res_out[6:8, :] = jnp.zeros((2, 256), F32)
    res_in[z] = res_out[...]

    def res_copy(r):
        return remote(res_out, res_in.at[z], rs_send.at[r], rs_recv.at[r], at_z(lax.rem(z + r, NZ)))

    for r in (4, 5, 3, 6, 2, 7, 1):
        res_copy(r).start()
    GR[...] = jnp.zeros_like(GR)

    def at_copy(j):
        r = lax.rem(j - z + NZ, NZ)
        return remote(at_out.at[j], at_in.at[z], at_send.at[r], at_recv.at[r], at_z(j))

    def yg_copy(h):
        return remote(yg_out.at[h], yg_in.at[h], yg_send.at[h], yg_recv.at[h], y_mate)

    for h in range(2):
        cols = slice(h * HS, h * HS + HS)
        wide = slice(h * 256, h * 256 + 256)

        def att2(r, _):
            j = lax.rem(z + NZ - r, NZ)
            if h == 0:

                @pl.when(r > 0)
                def _():
                    remote(res_out, res_in.at[j], rs_send.at[r], rs_recv.at[r], at_z(j)).wait_recv()

                @pl.when(r != 4)
                def _():
                    k = lax.rem(r + 4, NZ)
                    remote(st_out.at[j], far_in.at[j], far_send.at[k], far_recv.at[k], at_z(j)).wait_recv()

            tops = [ref[j, 3 * h : 3 * h + 1, :] for ref in (res_in, far_in)]
            top = jnp.maximum(tops[0], tops[1])
            fs = [jnp.exp(v - top) for v in tops]
            total, dots = [
                fs[0] * res_in[j, 3 * h + i : 3 * h + i + 1, :] + fs[1] * far_in[j, 3 * h + i : 3 * h + i + 1, :]
                for i in (1, 2)
            ]
            share = 1.0 / total
            p = E[j, h] * (jnp.exp(st_out[j, 3 * h : 3 * h + 1, :] - top) * share)
            rounded = p.astype(BF)
            ds = (p * (DP[j, h] - dots * share)).astype(BF)
            kg = dot(ds, G[j, 0, :, cols], NN) * scaling
            vg = dot(rounded, G[j, 1, :, cols], NN)
            part = jnp.concatenate([kg, vg], axis=1)
            for w in range(2):
                one = info_in[j, 2 + w : 3 + w, :]
                mine = part[w * CL : w * CL + CL]
                GR[w, 0:CL, wide] += mine * (1.0 - one)
                GR[w, CL : 2 * CL, wide] += mine * one
            values = chosen(j, h)[:, HS:]
            at_out[j, cols, :] = dot(values, rounded, TN).astype(BF)
            return 0

        lax.fori_loop(0, NZ, att2, 0)
        yg_out[h] = GR[1 - yh, :, wide].astype(BF)
        yg_copy(h).start()

    def at_start(r, _):
        at_copy(lax.rem(z + r, NZ)).start()
        return 0

    lax.fori_loop(1, NZ, at_start, 0)
    at_in[z] = at_out[z]

    def add_mate(h):
        wide = slice(h * 256, h * 256 + 256)
        yg_copy(h).wait_recv()
        kvg[:, wide] = (GR[yh, :, wide] + yg_in[h].astype(F32)).astype(BF)

    add_mate(0)

    two, nxt, prv = lax.rem(x + 2, NX), lax.rem(x + 1, NX), lax.rem(x + 3, NX)
    order = [two, nxt, prv, x]

    def w_rows(p, n, core):
        e = (order[n] * 2 + core) * 2 + (1 - m if p == 0 else m)
        return pl.ds(pl.multiple_of(e * 512, 512), 512)

    def half(p, n, core, h):
        wide = slice(h * 256, h * 256 + 256)
        return dot(kvg[:, wide], W[w_rows(p, n, core), wide], NT)

    early = {(0, 0, 0): 0, (0, 1, 0): 1, (0, 2, 0): 2, (0, 0, 1): 3}
    for (p, n, mine), i in early.items():
        PRE[i] = half(p, n, c if mine else 1 - c, 0)
    add_mate(1)

    def product(p, n, mine):
        core = c if mine else 1 - c
        if (p, n, mine) in early:
            return PRE[early[p, n, mine]] + half(p, n, core, 1)
        return dot(kvg[...], W[w_rows(p, n, core), :], NT)

    def cs_copy(p, n):
        return remote(cs_out.at[p, n], cs_in.at[p, n], cs_send.at[p, n], cs_recv.at[p, n], core_mate)

    def for_mate(p, n):
        cs_out[p, n] = product(p, n, 0).astype(BF)
        cs_copy(p, n).start()

    def own(p, n):
        mine = product(p, n, 1)
        cs_copy(p, n).wait_recv()
        R[p, n] = (mine + cs_in[p, n].astype(F32)).astype(BF)

    def by_copy(n):
        return remote(R.at[0, n, ROWS_A:256, :], by_in.at[n], by_send.at[n], by_recv.at[n], m_mate)

    def xsum(src, tmp, into, ssem, rsem):
        def at(n, half):
            return src(n, slice(half * 256, half * 256 + 256))

        firsts = [
            remote(at(0, 0), into.at[0], ssem.at[0], rsem.at[0], x_right),
            remote(at(0, 1), into.at[1], ssem.at[1], rsem.at[1], x_left),
            remote(at(1, 1), into.at[2], ssem.at[2], rsem.at[2], x_right),
            remote(at(2, 0), into.at[3], ssem.at[3], rsem.at[3], x_left),
        ]
        seconds = [
            remote(tmp.at[0], into.at[4], ssem.at[4], rsem.at[4], x_right),
            remote(tmp.at[1], into.at[5], ssem.at[5], rsem.at[5], x_left),
        ]

        def start(n):
            for i in [(0, 1), (2,), (3,), ()][n]:
                firsts[i].start()

        def relay():
            for i in range(2):
                firsts[i].wait_recv()
                tmp[i] = (at(1 + i, i)[...].astype(F32) + into[i].astype(F32)).astype(BF)
                seconds[i].start()

        def finish():
            firsts[2].wait_recv()
            firsts[3].wait_recv()
            seconds[0].wait_recv()
            seconds[1].wait_recv()
            halves = []
            for half, got in [(0, (4, 3)), (1, (2, 5))]:
                v = at(3, half)[...].astype(F32)
                for g in got:
                    v += into[g].astype(F32)
                halves.append(v)
            return halves

        def drain():
            for cp in firsts + seconds:
                cp.wait_send()

        return start, relay, finish, drain

    a0_start, a0_relay, a0_finish, a0_drain = xsum(
        lambda n, cols: R.at[0, n, 0:ROWS_A, cols],
        ax_tmp.at[0], ax_in.at[0], ax_send.at[0], ax_recv.at[0],
    )
    a1_start, a1_relay, a1_finish, a1_drain = xsum(
        lambda n, cols: R.at[1, n, 0:ROWS_A, cols],
        ax_tmp.at[1], ax_in.at[1], ax_send.at[1], ax_recv.at[1],
    )
    b_start, b_relay, b_finish, b_drain = xsum(
        lambda n, cols: RB.at[n, :, cols], bx_tmp, bx_in, bx_send, bx_recv
    )

    def add_b(n):
        by_copy(n).wait_recv()
        RB[n] = (R[1, n, ROWS_A:256, :].astype(F32) + by_in[n].astype(F32)).astype(BF)
        b_start(n)

    ay = remote(ay_out, ay_in, ay_send, ay_recv, m_mate)
    for_mate(0, 0)
    for_mate(0, 1)
    for_mate(0, 2)
    for n in range(NX):
        own(0, n)
        a0_start(n)
        by_copy(n).start()
        for_mate(*((0, 3) if n == 0 else (1, n - 1)))
    a0_relay()
    for n in range(NX):
        own(1, n)
        a1_start(n)
        if n == 0:
            for_mate(1, 3)
    add_b(0)
    fa = a0_finish()
    for half_ in range(2):
        ay_out[:, half_ * 256 : half_ * 256 + 256] = fa[half_].astype(BF)
    ay.start()
    a1_relay()
    add_b(1)
    add_b(2)
    b_relay()
    add_b(3)

    def at_wait(r, _):
        src = lax.rem(z + NZ - r, NZ)
        remote(at_out.at[src], at_in.at[src], at_send.at[r], at_recv.at[r], at_z(src)).wait_recv()
        return 0

    lax.fori_loop(1, NZ, at_wait, 0)
    total = at_in[0].astype(F32)
    for i in range(1, NZ):
        total += at_in[i].astype(F32)
    att_ref[...] = total.T.astype(BF)

    fb = b_finish()
    for half in range(2):
        cols = slice(half * 256, half * 256 + 256)
        nbr_ref[ROWS_A:256, cols] = fb[half].astype(BF)
    fa = a1_finish()
    ay.wait_recv()
    for half in range(2):
        cols = slice(half * 256, half * 256 + 256)
        nbr_ref[0:ROWS_A, cols] = (fa[half] + ay_in[:, cols].astype(F32)).astype(BF)

    for direction in range(2):
        for u in range(4):
            for t in range(4 if u < 2 else 3):
                ag(direction, u, t).wait_send()
    for h in range(2):
        kv_copy(h).wait_send()

    def sent(r, _):
        j = lax.rem(z + r, NZ)
        info_copy(r).wait_send()
        res_copy(r).wait_send()
        far_copy(r).wait_send()
        at_copy(j).wait_send()
        return 0

    lax.fori_loop(1, NZ, sent, 0)
    for r in near[1:]:
        st_copy(lax.rem(z + r, NZ)).wait_send()
    for h in range(2):
        yg_copy(h).wait_send()

    for n in range(NX):
        for p in range(2):
            cs_copy(p, n).wait_send()
        by_copy(n).wait_send()
    ay.wait_send()
    a0_drain()
    a1_drain()
    b_drain()


def on_device(nbr_states, kv_weight, queries, out_grad, citations):
    width = kv_weight.shape[0]
    rest = 256 - ROWS_A
    weight = kv_weight.reshape(width, 2, 2, HS).transpose(0, 2, 1, 3).reshape(width * 4, HS)
    V, D = pltpu.VMEM, pltpu.SemaphoreType.DMA
    scratch = [
        V((KC, 256, width // KC), BF),
        V((KC, width * 4 // KC, HS), BF),
        V((width, 512), BF),
        V((256, 256), F32),
        V((NZ, 2, 256, 256), BF),
        V((2, 2, 256, 256), BF),
        V((NZ, 8, 256), F32),
        V((NZ, 8, 256), F32),
        V((NZ, 2, 256, 256), F32),
        V((NZ, 2, 256, 256), F32),
        V((NZ, 8, 256), F32),
        V((NZ, 8, 256), F32),
        V((8, 256), F32),
        V((NZ, 8, 256), F32),
        V((NZ, 8, 256), F32),
        V((NZ, 256, 256), BF),
        V((NZ, 256, 256), BF),
        V((2, 256, 512), F32),
        V((2, 256, 256), BF),
        V((2, 256, 256), BF),
        V((256, 512), BF),
        V((2, NX, 256, 512), BF),
        V((2, NX, 256, 512), BF),
        V((2, NX, 256, 512), BF),
        V((NX, rest, 512), BF),
        V((NX, rest, 512), BF),
        V((2, 6, ROWS_A, 256), BF),
        V((2, 2, ROWS_A, 256), BF),
        V((6, rest, 256), BF),
        V((2, rest, 256), BF),
        V((ROWS_A, 512), BF),
        V((ROWS_A, 512), BF),
        V((256, 256), BF),
        V((4, 256, 512), F32),
        D((2, KC)),
        D((2,)),
        D((2, 4, 4)), D((2, 4, 4)),
        D((2,)), D((2,)),
        D((NZ,)), D((NZ,)),
        D((NZ,)), D((NZ,)),
        D((NZ,)), D((NZ,)),
        D((NZ,)), D((NZ,)),
        D((NZ,)), D((NZ,)),
        D((2,)), D((2,)),
        D((2, NX)), D((2, NX)),
        D((NX,)), D((NX,)),
        D((2, 6)), D((2, 6)),
        D((6,)), D((6,)),
        D, D,
    ]
    vmem = pl.BlockSpec(memory_space=pltpu.VMEM)
    hbm = pl.BlockSpec(memory_space=pl.ANY)
    return pl.pallas_call(
        kernel,
        out_shape=(pltpu.VMEM((256, 256), BF), pltpu.VMEM((256, 512), BF)),
        in_specs=[pl.BlockSpec(memory_space=pltpu.SMEM), hbm, hbm, hbm, hbm],
        out_specs=(vmem, vmem),
        scratch_shapes=scratch,
        compiler_params=pltpu.CompilerParams(
            collective_id=0, has_side_effects=True, vmem_limit_bytes=56 * 2**20
        ),
        cost_estimate=pl.CostEstimate(
            flops=6 * 10**9, bytes_accessed=13 * 2**20, transcendentals=2 * 10**6
        ),
    )(citations.T, queries, out_grad, nbr_states, weight)


def solution(mesh):
    heads = ("section", "mp")
    return jax.shard_map(
        on_device,
        mesh=mesh,
        in_specs=(
            P("dp", None),
            P(None, None, heads),
            P("dp", heads),
            P("dp", heads),
            P("dp", None),
        ),
        out_specs=(P("dp", heads), P("dp", heads)),
        check_vma=False,
    )
```

```python
import functools

import jax
import jax.numpy as jnp
from jax import lax
from jax.experimental import pallas as pl
from jax.experimental.pallas import tpu as pltpu
from jax.sharding import PartitionSpec as P

HS = 128
CH = 64
CL = 128
NZ = 8
NX = 4
KC = 8
ROWS_A = 144
NEG = -1e30
BF = jnp.bfloat16
F32 = jnp.float32
NT = (((1,), (1,)), ((), ()))
NN = (((1,), (0,)), ((), ()))
TN = (((0,), (0,)), ((), ()))


def dot(a, b, dims):
    return lax.dot_general(a, b, dims, preferred_element_type=F32)


def kernel(
    cit_ref, q_hbm, g_hbm, x_hbm, w_hbm, att_ref, nbr_ref,
    X, W32, W, acc, G, KV, info_out, info_in, E, DP, st_out, st_in, res_out, res_in,
    far_in, at_out, at_in, GR, yg_out, yg_in, kvg, cs_out, cs_in, R, by_in, RB,
    ax_in, ax_tmp, bx_in, bx_tmp, ay_out, ay_in, PM, PRE,
    ld_sem, own_sem, ag_send, ag_recv, kv_send, kv_recv, inf_send, inf_recv, st_send, st_recv,
    rs_send, rs_recv, far_send, far_recv, at_send, at_recv, yg_send, yg_recv, cs_send, cs_recv,
    by_send, by_recv, ax_send, ax_recv, bx_send, bx_recv, ay_send, ay_recv,
):
    s, d, m = lax.axis_index("section"), lax.axis_index("dp"), lax.axis_index("mp")
    x, c = s // 2, s % 2
    yh, z = d // NZ, d % NZ
    depth = x_hbm.shape[1] // KC
    scaling = 1.0 / HS**0.5

    def at_z(zt):
        return {"dp": yh * NZ + zt}

    y_mate = {"dp": (1 - yh) * NZ + z}
    core_mate = {"section": x * 2 + (1 - c)}
    x_right = {"section": lax.rem(x + 1, NX) * 2 + c}
    x_left = {"section": lax.rem(x + NX - 1, NX) * 2 + c}
    m_mate = {"mp": 1 - m}

    def remote(src, dst, ssem, rsem, dev):
        return pltpu.make_async_remote_copy(
            src_ref=src, dst_ref=dst, send_sem=ssem, recv_sem=rsem,
            device_id=dev, device_id_type=pl.DeviceIdType.MESH,
        )

    barrier = pltpu.get_barrier_semaphore()
    for dev in [at_z(lax.rem(z + r, NZ)) for r in range(1, NZ)] + [
        y_mate, core_mate, x_right, x_left, m_mate
    ]:
        pl.semaphore_signal(barrier, inc=1, device_id=dev, device_id_type=pl.DeviceIdType.MESH)

    def x_load(k):
        return pltpu.make_async_copy(
            x_hbm.at[:, pl.ds(pl.multiple_of(k * depth, depth), depth)], X.at[k], ld_sem.at[1, k]
        )

    def w_load(k):
        return pltpu.make_async_copy(
            w_hbm.at[pl.ds(pl.multiple_of(k * 4 * depth, depth), 4 * depth), :], W32.at[k], ld_sem.at[0, k]
        )

    own_rows = [pltpu.make_async_copy(src, G.at[z, i], own_sem.at[i]) for i, src in enumerate([q_hbm, g_hbm])]
    for cp in own_rows:
        cp.start()

    def start_loads(k, _):
        w_load(k).start()
        x_load(k).start()
        return 0

    lax.fori_loop(0, KC, start_loads, 0)

    for cp in own_rows:
        cp.wait()
    pl.semaphore_wait(barrier, 12)

    def ag(direction, u, t):
        if direction == 0:
            home, to, arr = lax.rem(z - t + NZ, NZ), lax.rem(z + 1, NZ), u // 2
        else:
            home, to, arr = lax.rem(z + t, NZ), lax.rem(z + NZ - 1, NZ), 1 - u // 2
        piece = G.at[home, arr, pl.ds(pl.multiple_of((u % 2) * 128, 128), 128)]
        return remote(piece, piece, ag_send.at[direction, u, t], ag_recv.at[direction, u, t], at_z(to))

    for u in range(4):
        for direction in range(2):
            ag(direction, u, 0).start()

    lane = lax.broadcasted_iota(jnp.int32, (16, 256), 1) // CH
    owner = lax.broadcasted_iota(jnp.int32, (16, 256), 0)
    ids = []
    for k in range(2):
        v = jnp.zeros((16, 256), jnp.int32)
        for b in range(4):
            v = jnp.where(lane == b, cit_ref[k, b], v)
        ids.append(v)
    second = (ids[0] == owner * 2 + 1) | (ids[1] == owner * 2 + 1)
    first = (ids[0] == owner * 2) | (ids[1] == owner * 2)
    cited = jnp.where(first | second, 1.0, 0.0).astype(F32)
    sel = jnp.where(second, 1.0, 0.0).astype(F32)
    sel = jnp.max(sel, axis=1, keepdims=True) + jnp.zeros((16, 256), F32)
    for t in range(NZ):
        for w in range(2):
            o = w * NZ + t
            info_out[t, w : w + 1, :] = cited[o : o + 1]
            info_out[t, 2 + w : 3 + w, :] = sel[o : o + 1]
        info_out[t, 4:8, :] = jnp.zeros((4, 256), F32)
    info_in[z] = info_out[z]
    def info_copy(r):
        to = lax.rem(z + r, NZ)
        return remote(info_out.at[to], info_in.at[z], inf_send.at[r], inf_recv.at[r], at_z(to))

    def info_start(r, _):
        info_copy(r).start()
        return 0

    lax.fori_loop(1, NZ, info_start, 0)

    def relay(t, u):
        for direction in range(2):
            ag(direction, u, t - 1).wait_recv()
            ag(direction, u, t).start()

    def arrived(t, u):
        for direction in range(2):
            ag(direction, u, t).wait_recv()

    out_row = lax.broadcasted_iota(jnp.int32, (256, 256), 0)
    in_row = lax.broadcasted_iota(jnp.int32, (256, 256), 1)
    PM[...] = jnp.where(in_row == (out_row % 64) * 4 + out_row // 64, 1.0, 0.0).astype(BF)

    def piece(k, _):
        w_load(k).wait()

        def sort(i, _):
            for u in range(4):
                b = i * 4 + u
                got = dot(PM[...], W32[k, pl.ds(pl.multiple_of(b * 256, 256), 256), :], NN).astype(BF)
                rows = pl.ds(pl.multiple_of(k * depth + b * 64, 64), 64)
                for n in range(4):
                    W[rows, n * HS : n * HS + HS] = got[n * 64 : n * 64 + 64]
            return 0

        lax.fori_loop(0, depth // 256, sort, 0)
        x_load(k).wait()
        rows = pl.ds(pl.multiple_of(k * depth, depth), depth)
        acc[...] += dot(X[k], W[rows, 0:256], NN)

        @pl.when(k >= 2)
        def _():
            relay(1 + (k - 2) // 4, (k - 2) % 4)

        return 0

    def piece_1(k, _):
        rows = pl.ds(pl.multiple_of(k * depth, depth), depth)
        acc[...] += dot(X[k], W[rows, 256:512], NN)
        return 0

    def kv_copy(h):
        return remote(KV.at[yh, h], KV.at[yh, h], kv_send.at[h], kv_recv.at[h], y_mate)

    for h, body in enumerate([piece, piece_1]):
        acc[...] = jnp.zeros_like(acc)
        lax.fori_loop(0, KC, body, 0)
        KV[yh, h] = acc[...].astype(BF)
        kv_copy(h).start()

    def kv_wait(h):
        pltpu.make_async_remote_copy(
            src_ref=KV.at[1 - yh, h], dst_ref=KV.at[1 - yh, h], send_sem=kv_send.at[h],
            recv_sem=kv_recv.at[h], device_id=y_mate, device_id_type=pl.DeviceIdType.MESH,
        ).wait_recv()

    def info_wait(r, _):
        info_copy(r).wait_recv()
        return 0

    relay(2, 2)
    relay(2, 3)
    lax.fori_loop(1, NZ, info_wait, 0)
    relay(3, 0)
    relay(3, 1)
    kv_wait(0)

    def chosen(j, h):
        out = []
        for w in range(2):
            f = info_in[j, 2 + w : 3 + w, :] + jnp.zeros((CL, 256), F32)
            one, zero = f.astype(BF), (1.0 - f).astype(BF)
            out.append(KV[w, h, 0:CL, :] * zero + KV[w, h, CL : 2 * CL, :] * one)
        return jnp.concatenate(out, axis=0)

    def st_copy(j):
        r = lax.rem(j - z + NZ, NZ)
        return remote(st_out.at[j], st_in.at[z], st_send.at[r], st_recv.at[r], at_z(j))

    def att1(j, heads=(0, 1)):
        for h in heads:
            kv = chosen(j, h)
            cols = slice(h * HS, h * HS + HS)
            sc = dot(kv[:, :HS], G[j, 0, :, cols], NT) * scaling
            sc = jnp.concatenate(
                [
                    jnp.where(info_in[j, w : w + 1, :] > 0.0, sc[w * CL : w * CL + CL], NEG)
                    for w in range(2)
                ],
                axis=0,
            )
            top = jnp.max(sc, axis=0, keepdims=True)
            e = jnp.exp(sc - top)
            dp = dot(kv[:, HS:], G[j, 1, :, cols], NT)
            E[j, h] = e
            DP[j, h] = dp
            st_out[j, 3 * h : 3 * h + 1, :] = top
            st_out[j, 3 * h + 1 : 3 * h + 2, :] = jnp.sum(e, axis=0, keepdims=True)
            st_out[j, 3 * h + 2 : 3 * h + 3, :] = jnp.sum(e * dp, axis=0, keepdims=True)
        if 1 in heads:
            st_out[j, 6:8, :] = jnp.zeros((2, 256), F32)

    def both(t, heads=(0, 1)):
        def side(i, _):
            j = lax.rem(z + NZ - t + 2 * i * t, NZ)
            att1(j, heads)
            if 1 in heads:
                st_copy(j).start()
            return 0

        lax.fori_loop(0, 2, side, 0)

    far = lax.rem(z + 4, NZ)

    def far_copy(r):
        return remote(st_out.at[far], far_in.at[far], far_send.at[r], far_recv.at[r], at_z(lax.rem(z + r, NZ)))

    att1(z, (0,))
    both(1, (0,))
    both(2, (0,))
    kv_wait(1)
    both(2, (1,))
    arrived(2, 2)
    arrived(2, 3)
    both(3)
    both(1, (1,))
    att1(z, (1,))
    arrived(3, 0)
    arrived(3, 1)
    att1(far)
    far_in[far] = st_out[far]
    for r in (4, 5, 3, 6, 2, 7, 1):
        far_copy(r).start()

    near = (0, 1, 2, 3, 5, 6, 7)
    st_in[z] = st_out[z]
    for r in near[1:]:
        src = lax.rem(z + NZ - r, NZ)
        remote(st_out.at[src], st_in.at[src], st_send.at[r], st_recv.at[r], at_z(src)).wait_recv()
    for h in range(2):
        stats = [[st_in[lax.rem(z + NZ - r, NZ), 3 * h + i : 3 * h + i + 1, :] for i in range(3)] for r in near]
        top = functools.reduce(jnp.maximum, [v[0] for v in stats])
        total = jnp.zeros((1, 256), F32)
        dots = jnp.zeros((1, 256), F32)
        for v in stats:
            f = jnp.exp(v[0] - top)
            total += f * v[1]
            dots += f * v[2]
        res_out[3 * h : 3 * h + 1, :] = top
        res_out[3 * h + 1 : 3 * h + 2, :] = total
        res_out[3 * h + 2 : 3 * h + 3, :] = dots
    res_out[6:8, :] = jnp.zeros((2, 256), F32)
    res_in[z] = res_out[...]

    def res_copy(r):
        return remote(res_out, res_in.at[z], rs_send.at[r], rs_recv.at[r], at_z(lax.rem(z + r, NZ)))

    for r in (4, 5, 3, 6, 2, 7, 1):
        res_copy(r).start()
    GR[...] = jnp.zeros_like(GR)

    def at_copy(j):
        r = lax.rem(j - z + NZ, NZ)
        return remote(at_out.at[j], at_in.at[z], at_send.at[r], at_recv.at[r], at_z(j))

    def yg_copy(h):
        return remote(yg_out.at[h], yg_in.at[h], yg_send.at[h], yg_recv.at[h], y_mate)

    for h in range(2):
        cols = slice(h * HS, h * HS + HS)
        wide = slice(h * 256, h * 256 + 256)

        def att2(r, _):
            j = lax.rem(z + NZ - r, NZ)
            if h == 0:

                @pl.when(r > 0)
                def _():
                    remote(res_out, res_in.at[j], rs_send.at[r], rs_recv.at[r], at_z(j)).wait_recv()

                @pl.when(r != 4)
                def _():
                    k = lax.rem(r + 4, NZ)
                    remote(st_out.at[j], far_in.at[j], far_send.at[k], far_recv.at[k], at_z(j)).wait_recv()

            tops = [ref[j, 3 * h : 3 * h + 1, :] for ref in (res_in, far_in)]
            top = jnp.maximum(tops[0], tops[1])
            fs = [jnp.exp(v - top) for v in tops]
            total, dots = [
                fs[0] * res_in[j, 3 * h + i : 3 * h + i + 1, :] + fs[1] * far_in[j, 3 * h + i : 3 * h + i + 1, :]
                for i in (1, 2)
            ]
            share = 1.0 / total
            p = E[j, h] * (jnp.exp(st_out[j, 3 * h : 3 * h + 1, :] - top) * share)
            rounded = p.astype(BF)
            ds = (p * (DP[j, h] - dots * share)).astype(BF)
            kg = dot(ds, G[j, 0, :, cols], NN) * scaling
            vg = dot(rounded, G[j, 1, :, cols], NN)
            part = jnp.concatenate([kg, vg], axis=1)
            for w in range(2):
                one = info_in[j, 2 + w : 3 + w, :]
                mine = part[w * CL : w * CL + CL]
                GR[w, 0:CL, wide] += mine * (1.0 - one)
                GR[w, CL : 2 * CL, wide] += mine * one
            values = chosen(j, h)[:, HS:]
            at_out[j, cols, :] = dot(values, rounded, TN).astype(BF)
            return 0

        lax.fori_loop(0, NZ, att2, 0)
        yg_out[h] = GR[1 - yh, :, wide].astype(BF)
        yg_copy(h).start()

    def at_start(r, _):
        at_copy(lax.rem(z + r, NZ)).start()
        return 0

    lax.fori_loop(1, NZ, at_start, 0)
    at_in[z] = at_out[z]

    def add_mate(h):
        wide = slice(h * 256, h * 256 + 256)
        yg_copy(h).wait_recv()
        kvg[:, wide] = (GR[yh, :, wide] + yg_in[h].astype(F32)).astype(BF)

    for direction in range(2):
        for u in range(4):
            for t in range(4 if u < 2 else 3):
                ag(direction, u, t).wait_send()
    for h in range(2):
        kv_copy(h).wait_send()

    def sent(r, _):
        info_copy(r).wait_send()
        res_copy(r).wait_send()
        far_copy(r).wait_send()
        return 0

    lax.fori_loop(1, NZ, sent, 0)
    for r in near[1:]:
        st_copy(lax.rem(z + r, NZ)).wait_send()
    add_mate(0)

    two, nxt, prv = lax.rem(x + 2, NX), lax.rem(x + 1, NX), lax.rem(x + 3, NX)
    order = [two, nxt, prv, x]

    def w_rows(p, n, core):
        e = (order[n] * 2 + core) * 2 + (1 - m if p == 0 else m)
        return pl.ds(pl.multiple_of(e * 512, 512), 512)

    def half(p, n, core, h):
        wide = slice(h * 256, h * 256 + 256)
        return dot(kvg[:, wide], W[w_rows(p, n, core), wide], NT)

    early = {(0, 0, 0): 0, (0, 1, 0): 1, (0, 2, 0): 2, (0, 0, 1): 3}
    for (p, n, mine), i in early.items():
        PRE[i] = half(p, n, c if mine else 1 - c, 0)
    add_mate(1)

    def product(p, n, mine):
        core = c if mine else 1 - c
        if (p, n, mine) in early:
            return PRE[early[p, n, mine]] + half(p, n, core, 1)
        return dot(kvg[...], W[w_rows(p, n, core), :], NT)

    def cs_copy(p, n):
        return remote(cs_out.at[p, n], cs_in.at[p, n], cs_send.at[p, n], cs_recv.at[p, n], core_mate)

    def for_mate(p, n):
        cs_out[p, n] = product(p, n, 0).astype(BF)
        cs_copy(p, n).start()

    def own(p, n):
        mine = product(p, n, 1)
        cs_copy(p, n).wait_recv()
        R[p, n] = (mine + cs_in[p, n].astype(F32)).astype(BF)

    def by_copy(n):
        return remote(R.at[0, n, ROWS_A:256, :], by_in.at[n], by_send.at[n], by_recv.at[n], m_mate)

    def xsum(src, tmp, into, ssem, rsem):
        def at(n, half):
            return src(n, slice(half * 256, half * 256 + 256))

        firsts = [
            remote(at(0, 0), into.at[0], ssem.at[0], rsem.at[0], x_right),
            remote(at(0, 1), into.at[1], ssem.at[1], rsem.at[1], x_left),
            remote(at(1, 1), into.at[2], ssem.at[2], rsem.at[2], x_right),
            remote(at(2, 0), into.at[3], ssem.at[3], rsem.at[3], x_left),
        ]
        seconds = [
            remote(tmp.at[0], into.at[4], ssem.at[4], rsem.at[4], x_right),
            remote(tmp.at[1], into.at[5], ssem.at[5], rsem.at[5], x_left),
        ]

        def start(n):
            for i in [(0, 1), (2,), (3,), ()][n]:
                firsts[i].start()

        def relay():
            for i in range(2):
                firsts[i].wait_recv()
                tmp[i] = (at(1 + i, i)[...].astype(F32) + into[i].astype(F32)).astype(BF)
                seconds[i].start()

        def finish():
            firsts[2].wait_recv()
            firsts[3].wait_recv()
            seconds[0].wait_recv()
            seconds[1].wait_recv()
            halves = []
            for half, got in [(0, (4, 3)), (1, (2, 5))]:
                v = at(3, half)[...].astype(F32)
                for g in got:
                    v += into[g].astype(F32)
                halves.append(v)
            return halves

        def drain():
            for cp in firsts + seconds:
                cp.wait_send()

        return start, relay, finish, drain

    a0_start, a0_relay, a0_finish, a0_drain = xsum(
        lambda n, cols: R.at[0, n, 0:ROWS_A, cols],
        ax_tmp.at[0], ax_in.at[0], ax_send.at[0], ax_recv.at[0],
    )
    a1_start, a1_relay, a1_finish, a1_drain = xsum(
        lambda n, cols: R.at[1, n, 0:ROWS_A, cols],
        ax_tmp.at[1], ax_in.at[1], ax_send.at[1], ax_recv.at[1],
    )
    b_start, b_relay, b_finish, b_drain = xsum(
        lambda n, cols: RB.at[n, :, cols], bx_tmp, bx_in, bx_send, bx_recv
    )

    def add_b(n):
        by_copy(n).wait_recv()
        RB[n] = (R[1, n, ROWS_A:256, :].astype(F32) + by_in[n].astype(F32)).astype(BF)
        b_start(n)

    ay = remote(ay_out, ay_in, ay_send, ay_recv, m_mate)
    for_mate(0, 0)
    for_mate(0, 1)
    for_mate(0, 2)
    for n in range(NX):
        own(0, n)
        a0_start(n)
        by_copy(n).start()
        for_mate(*((0, 3) if n == 0 else (1, n - 1)))
    a0_relay()
    for n in range(NX):
        own(1, n)
        a1_start(n)
        if n == 0:
            for_mate(1, 3)
    add_b(0)
    fa = a0_finish()
    for half_ in range(2):
        ay_out[:, half_ * 256 : half_ * 256 + 256] = fa[half_].astype(BF)
    ay.start()
    a1_relay()
    add_b(1)
    add_b(2)
    b_relay()
    add_b(3)

    def at_wait(r, _):
        src = lax.rem(z + NZ - r, NZ)
        remote(at_out.at[src], at_in.at[src], at_send.at[r], at_recv.at[r], at_z(src)).wait_recv()
        return 0

    lax.fori_loop(1, NZ, at_wait, 0)
    total = at_in[0].astype(F32)
    for i in range(1, NZ):
        total += at_in[i].astype(F32)
    att_ref[...] = total.T.astype(BF)

    def at_sent(r, _):
        at_copy(lax.rem(z + r, NZ)).wait_send()
        return 0

    lax.fori_loop(1, NZ, at_sent, 0)
    for h in range(2):
        yg_copy(h).wait_send()

    for n in range(NX):
        for p in range(2):
            cs_copy(p, n).wait_send()
        by_copy(n).wait_send()
    fb = b_finish()
    for half in range(2):
        cols = slice(half * 256, half * 256 + 256)
        nbr_ref[ROWS_A:256, cols] = fb[half].astype(BF)
    fa = a1_finish()
    ay.wait_recv()
    for half in range(2):
        cols = slice(half * 256, half * 256 + 256)
        nbr_ref[0:ROWS_A, cols] = (fa[half] + ay_in[:, cols].astype(F32)).astype(BF)

    ay.wait_send()
    a0_drain()
    a1_drain()
    b_drain()


def on_device(nbr_states, kv_weight, queries, out_grad, citations):
    width = kv_weight.shape[0]
    rest = 256 - ROWS_A
    weight = kv_weight.reshape(width, 2, 2, HS).transpose(0, 2, 1, 3).reshape(width * 4, HS)
    V, D = pltpu.VMEM, pltpu.SemaphoreType.DMA
    scratch = [
        V((KC, 256, width // KC), BF),
        V((KC, width * 4 // KC, HS), BF),
        V((width, 512), BF),
        V((256, 256), F32),
        V((NZ, 2, 256, 256), BF),
        V((2, 2, 256, 256), BF),
        V((NZ, 8, 256), F32),
        V((NZ, 8, 256), F32),
        V((NZ, 2, 256, 256), F32),
        V((NZ, 2, 256, 256), F32),
        V((NZ, 8, 256), F32),
        V((NZ, 8, 256), F32),
        V((8, 256), F32),
        V((NZ, 8, 256), F32),
        V((NZ, 8, 256), F32),
        V((NZ, 256, 256), BF),
        V((NZ, 256, 256), BF),
        V((2, 256, 512), F32),
        V((2, 256, 256), BF),
        V((2, 256, 256), BF),
        V((256, 512), BF),
        V((2, NX, 256, 512), BF),
        V((2, NX, 256, 512), BF),
        V((2, NX, 256, 512), BF),
        V((NX, rest, 512), BF),
        V((NX, rest, 512), BF),
        V((2, 6, ROWS_A, 256), BF),
        V((2, 2, ROWS_A, 256), BF),
        V((6, rest, 256), BF),
        V((2, rest, 256), BF),
        V((ROWS_A, 512), BF),
        V((ROWS_A, 512), BF),
        V((256, 256), BF),
        V((4, 256, 512), F32),
        D((2, KC)),
        D((2,)),
        D((2, 4, 4)), D((2, 4, 4)),
        D((2,)), D((2,)),
        D((NZ,)), D((NZ,)),
        D((NZ,)), D((NZ,)),
        D((NZ,)), D((NZ,)),
        D((NZ,)), D((NZ,)),
        D((NZ,)), D((NZ,)),
        D((2,)), D((2,)),
        D((2, NX)), D((2, NX)),
        D((NX,)), D((NX,)),
        D((2, 6)), D((2, 6)),
        D((6,)), D((6,)),
        D, D,
    ]
    vmem = pl.BlockSpec(memory_space=pltpu.VMEM)
    hbm = pl.BlockSpec(memory_space=pl.ANY)
    return pl.pallas_call(
        kernel,
        out_shape=(pltpu.VMEM((256, 256), BF), pltpu.VMEM((256, 512), BF)),
        in_specs=[pl.BlockSpec(memory_space=pltpu.SMEM), hbm, hbm, hbm, hbm],
        out_specs=(vmem, vmem),
        scratch_shapes=scratch,
        compiler_params=pltpu.CompilerParams(
            collective_id=0, has_side_effects=True, vmem_limit_bytes=56 * 2**20
        ),
        cost_estimate=pl.CostEstimate(
            flops=6 * 10**9, bytes_accessed=13 * 2**20, transcendentals=2 * 10**6
        ),
    )(citations.T, queries, out_grad, nbr_states, weight)


def solution(mesh):
    heads = ("section", "mp")
    return jax.shard_map(
        on_device,
        mesh=mesh,
        in_specs=(
            P("dp", None),
            P(None, None, heads),
            P("dp", heads),
            P("dp", heads),
            P("dp", None),
        ),
        out_specs=(P("dp", heads), P("dp", heads)),
        check_vma=False,
    )
```

```python
import functools

import jax
import jax.numpy as jnp
from jax import lax
from jax.experimental import pallas as pl
from jax.experimental.pallas import tpu as pltpu
from jax.sharding import PartitionSpec as P

HS = 128
CH = 64
CL = 128
NZ = 8
NX = 4
KC = 8
ROWS_A = 144
NEG = -1e30
BF = jnp.bfloat16
F32 = jnp.float32
NT = (((1,), (1,)), ((), ()))
NN = (((1,), (0,)), ((), ()))
TN = (((0,), (0,)), ((), ()))


def dot(a, b, dims):
    return lax.dot_general(a, b, dims, preferred_element_type=F32)


def kernel(
    cit_ref, q_hbm, g_hbm, x_hbm, w_hbm, att_ref, nbr_ref,
    X, W32, W, acc, G, KV, info_out, info_in, E, DP, st_out, st_in, res_out, res_in,
    far_in, at_out, at_in, GR, yg_out, yg_in, kvg, cs_out, cs_in, R, by_in, RB,
    ax_in, ax_tmp, bx_in, bx_tmp, ay_out, ay_in, PM, PRE,
    ld_sem, own_sem, ag_send, ag_recv, kv_send, kv_recv, inf_send, inf_recv, st_send, st_recv,
    rs_send, rs_recv, far_send, far_recv, at_send, at_recv, yg_send, yg_recv, cs_send, cs_recv,
    by_send, by_recv, ax_send, ax_recv, bx_send, bx_recv, ay_send, ay_recv,
):
    s, d, m = lax.axis_index("section"), lax.axis_index("dp"), lax.axis_index("mp")
    x, c = s // 2, s % 2
    yh, z = d // NZ, d % NZ
    depth = x_hbm.shape[1] // KC
    scaling = 1.0 / HS**0.5

    def at_z(zt):
        return {"dp": yh * NZ + zt}

    y_mate = {"dp": (1 - yh) * NZ + z}
    core_mate = {"section": x * 2 + (1 - c)}
    x_right = {"section": lax.rem(x + 1, NX) * 2 + c}
    x_left = {"section": lax.rem(x + NX - 1, NX) * 2 + c}
    m_mate = {"mp": 1 - m}

    def remote(src, dst, ssem, rsem, dev):
        return pltpu.make_async_remote_copy(
            src_ref=src, dst_ref=dst, send_sem=ssem, recv_sem=rsem,
            device_id=dev, device_id_type=pl.DeviceIdType.MESH,
        )

    barrier = pltpu.get_barrier_semaphore()
    for dev in [at_z(lax.rem(z + r, NZ)) for r in range(1, NZ)] + [
        y_mate, core_mate, x_right, x_left, m_mate
    ]:
        pl.semaphore_signal(barrier, inc=1, device_id=dev, device_id_type=pl.DeviceIdType.MESH)

    def x_load(k):
        return pltpu.make_async_copy(
            x_hbm.at[:, pl.ds(pl.multiple_of(k * depth, depth), depth)], X.at[k], ld_sem.at[1, k]
        )

    def w_load(k):
        return pltpu.make_async_copy(
            w_hbm.at[pl.ds(pl.multiple_of(k * 4 * depth, depth), 4 * depth), :], W32.at[k], ld_sem.at[0, k]
        )

    own_rows = [pltpu.make_async_copy(src, G.at[z, i], own_sem.at[i]) for i, src in enumerate([q_hbm, g_hbm])]
    for cp in own_rows:
        cp.start()

    def start_loads(k, _):
        w_load(k).start()
        x_load(k).start()
        return 0

    lax.fori_loop(0, KC, start_loads, 0)

    for cp in own_rows:
        cp.wait()
    pl.semaphore_wait(barrier, 12)

    def ag(direction, u, t):
        if direction == 0:
            home, to, arr = lax.rem(z - t + NZ, NZ), lax.rem(z + 1, NZ), u // 2
        else:
            home, to, arr = lax.rem(z + t, NZ), lax.rem(z + NZ - 1, NZ), 1 - u // 2
        piece = G.at[home, arr, pl.ds(pl.multiple_of((u % 2) * 128, 128), 128)]
        return remote(piece, piece, ag_send.at[direction, u, t], ag_recv.at[direction, u, t], at_z(to))

    for u in range(4):
        for direction in range(2):
            ag(direction, u, 0).start()

    lane = lax.broadcasted_iota(jnp.int32, (16, 256), 1) // CH
    owner = lax.broadcasted_iota(jnp.int32, (16, 256), 0)
    ids = []
    for k in range(2):
        v = jnp.zeros((16, 256), jnp.int32)
        for b in range(4):
            v = jnp.where(lane == b, cit_ref[k, b], v)
        ids.append(v)
    second = (ids[0] == owner * 2 + 1) | (ids[1] == owner * 2 + 1)
    first = (ids[0] == owner * 2) | (ids[1] == owner * 2)
    cited = jnp.where(first | second, 1.0, 0.0).astype(F32)
    sel = jnp.where(second, 1.0, 0.0).astype(F32)
    sel = jnp.max(sel, axis=1, keepdims=True) + jnp.zeros((16, 256), F32)
    for t in range(NZ):
        for w in range(2):
            o = w * NZ + t
            info_out[t, w : w + 1, :] = cited[o : o + 1]
            info_out[t, 2 + w : 3 + w, :] = sel[o : o + 1]
        info_out[t, 4:8, :] = jnp.zeros((4, 256), F32)
    info_in[z] = info_out[z]
    def info_copy(r):
        to = lax.rem(z + r, NZ)
        return remote(info_out.at[to], info_in.at[z], inf_send.at[r], inf_recv.at[r], at_z(to))

    def info_start(r, _):
        info_copy(r).start()
        return 0

    lax.fori_loop(1, NZ, info_start, 0)

    def relay(t, u):
        for direction in range(2):
            ag(direction, u, t - 1).wait_recv()
            ag(direction, u, t).start()

    def arrived(t, u):
        for direction in range(2):
            ag(direction, u, t).wait_recv()

    out_row = lax.broadcasted_iota(jnp.int32, (256, 256), 0)
    in_row = lax.broadcasted_iota(jnp.int32, (256, 256), 1)
    PM[...] = jnp.where(in_row == (out_row % 64) * 4 + out_row // 64, 1.0, 0.0).astype(BF)

    def piece(k, _):
        w_load(k).wait()

        def sort(i, _):
            for u in range(4):
                b = i * 4 + u
                got = dot(PM[...], W32[k, pl.ds(pl.multiple_of(b * 256, 256), 256), :], NN).astype(BF)
                rows = pl.ds(pl.multiple_of(k * depth + b * 64, 64), 64)
                for n in range(4):
                    W[rows, n * HS : n * HS + HS] = got[n * 64 : n * 64 + 64]
            return 0

        lax.fori_loop(0, depth // 256, sort, 0)
        x_load(k).wait()
        rows = pl.ds(pl.multiple_of(k * depth, depth), depth)
        acc[...] += dot(X[k], W[rows, 0:256], NN)

        @pl.when(k >= 2)
        def _():
            relay(1 + (k - 2) // 4, (k - 2) % 4)

        return 0

    def piece_1(k, _):
        rows = pl.ds(pl.multiple_of(k * depth, depth), depth)
        acc[...] += dot(X[k], W[rows, 256:512], NN)
        return 0

    def kv_copy(h):
        return remote(KV.at[yh, h], KV.at[yh, h], kv_send.at[h], kv_recv.at[h], y_mate)

    for h, body in enumerate([piece, piece_1]):
        acc[...] = jnp.zeros_like(acc)
        lax.fori_loop(0, KC, body, 0)
        KV[yh, h] = acc[...].astype(BF)
        kv_copy(h).start()

    def kv_wait(h):
        pltpu.make_async_remote_copy(
            src_ref=KV.at[1 - yh, h], dst_ref=KV.at[1 - yh, h], send_sem=kv_send.at[h],
            recv_sem=kv_recv.at[h], device_id=y_mate, device_id_type=pl.DeviceIdType.MESH,
        ).wait_recv()

    def info_wait(r, _):
        info_copy(r).wait_recv()
        return 0

    relay(2, 2)
    relay(2, 3)
    lax.fori_loop(1, NZ, info_wait, 0)
    relay(3, 0)
    relay(3, 1)
    kv_wait(0)

    def chosen(j, h):
        out = []
        for w in range(2):
            f = info_in[j, 2 + w : 3 + w, :] + jnp.zeros((CL, 256), F32)
            one, zero = f.astype(BF), (1.0 - f).astype(BF)
            out.append(KV[w, h, 0:CL, :] * zero + KV[w, h, CL : 2 * CL, :] * one)
        return jnp.concatenate(out, axis=0)

    def st_copy(j):
        r = lax.rem(j - z + NZ, NZ)
        return remote(st_out.at[j], st_in.at[z], st_send.at[r], st_recv.at[r], at_z(j))

    def att1(j, heads=(0, 1)):
        for h in heads:
            kv = chosen(j, h)
            cols = slice(h * HS, h * HS + HS)
            sc = dot(kv[:, :HS], G[j, 0, :, cols], NT) * scaling
            sc = jnp.concatenate(
                [
                    jnp.where(info_in[j, w : w + 1, :] > 0.0, sc[w * CL : w * CL + CL], NEG)
                    for w in range(2)
                ],
                axis=0,
            )
            top = jnp.max(sc, axis=0, keepdims=True)
            e = jnp.exp(sc - top)
            dp = dot(kv[:, HS:], G[j, 1, :, cols], NT)
            E[j, h] = e
            DP[j, h] = dp
            st_out[j, 3 * h : 3 * h + 1, :] = top
            st_out[j, 3 * h + 1 : 3 * h + 2, :] = jnp.sum(e, axis=0, keepdims=True)
            st_out[j, 3 * h + 2 : 3 * h + 3, :] = jnp.sum(e * dp, axis=0, keepdims=True)
        if 1 in heads:
            st_out[j, 6:8, :] = jnp.zeros((2, 256), F32)

    def both(t, heads=(0, 1)):
        def side(i, _):
            j = lax.rem(z + NZ - t + 2 * i * t, NZ)
            att1(j, heads)
            if 1 in heads:
                st_copy(j).start()
            return 0

        lax.fori_loop(0, 2, side, 0)

    far = lax.rem(z + 4, NZ)

    def far_copy(r):
        return remote(st_out.at[far], far_in.at[far], far_send.at[r], far_recv.at[r], at_z(lax.rem(z + r, NZ)))

    att1(z, (0,))
    both(1, (0,))
    both(2, (0,))
    kv_wait(1)
    both(2, (1,))
    arrived(2, 2)
    arrived(2, 3)
    both(3)
    both(1, (1,))
    att1(z, (1,))
    arrived(3, 0)
    arrived(3, 1)
    att1(far)
    far_in[far] = st_out[far]
    for r in (4, 5, 3, 6, 2, 7, 1):
        far_copy(r).start()

    near = (0, 1, 2, 3, 5, 6, 7)
    st_in[z] = st_out[z]
    for r in near[1:]:
        src = lax.rem(z + NZ - r, NZ)
        remote(st_out.at[src], st_in.at[src], st_send.at[r], st_recv.at[r], at_z(src)).wait_recv()
    for h in range(2):
        stats = [[st_in[lax.rem(z + NZ - r, NZ), 3 * h + i : 3 * h + i + 1, :] for i in range(3)] for r in near]
        top = functools.reduce(jnp.maximum, [v[0] for v in stats])
        total = jnp.zeros((1, 256), F32)
        dots = jnp.zeros((1, 256), F32)
        for v in stats:
            f = jnp.exp(v[0] - top)
            total += f * v[1]
            dots += f * v[2]
        res_out[3 * h : 3 * h + 1, :] = top
        res_out[3 * h + 1 : 3 * h + 2, :] = total
        res_out[3 * h + 2 : 3 * h + 3, :] = dots
    res_out[6:8, :] = jnp.zeros((2, 256), F32)
    res_in[z] = res_out[...]

    def res_copy(r):
        return remote(res_out, res_in.at[z], rs_send.at[r], rs_recv.at[r], at_z(lax.rem(z + r, NZ)))

    for r in (4, 5, 3, 6, 2, 7, 1):
        res_copy(r).start()
    GR[...] = jnp.zeros_like(GR)

    def at_copy(j):
        r = lax.rem(j - z + NZ, NZ)
        return remote(at_out.at[j], at_in.at[z], at_send.at[r], at_recv.at[r], at_z(j))

    def yg_copy(h):
        return remote(yg_out.at[h], yg_in.at[h], yg_send.at[h], yg_recv.at[h], y_mate)

    for h in range(2):
        cols = slice(h * HS, h * HS + HS)
        wide = slice(h * 256, h * 256 + 256)

        def att2(i, _):
            pair = i // 2
            r = 2 + pair - 3 * (pair // 2) - 2 * (pair // 3) + 4 * (i % 2)
            j = lax.rem(z + NZ - r, NZ)
            if h == 0:

                @pl.when(r > 0)
                def _():
                    remote(res_out, res_in.at[j], rs_send.at[r], rs_recv.at[r], at_z(j)).wait_recv()

                @pl.when(r != 4)
                def _():
                    k = lax.rem(r + 4, NZ)
                    remote(st_out.at[j], far_in.at[j], far_send.at[k], far_recv.at[k], at_z(j)).wait_recv()

            tops = [ref[j, 3 * h : 3 * h + 1, :] for ref in (res_in, far_in)]
            top = jnp.maximum(tops[0], tops[1])
            fs = [jnp.exp(v - top) for v in tops]
            total, dots = [
                fs[0] * res_in[j, 3 * h + i : 3 * h + i + 1, :] + fs[1] * far_in[j, 3 * h + i : 3 * h + i + 1, :]
                for i in (1, 2)
            ]
            share = 1.0 / total
            p = E[j, h] * (jnp.exp(st_out[j, 3 * h : 3 * h + 1, :] - top) * share)
            rounded = p.astype(BF)
            ds = (p * (DP[j, h] - dots * share)).astype(BF)
            kg = dot(ds, G[j, 0, :, cols], NN) * scaling
            vg = dot(rounded, G[j, 1, :, cols], NN)
            part = jnp.concatenate([kg, vg], axis=1)
            for w in range(2):
                one = info_in[j, 2 + w : 3 + w, :]
                mine = part[w * CL : w * CL + CL]
                GR[w, 0:CL, wide] += mine * (1.0 - one)
                GR[w, CL : 2 * CL, wide] += mine * one
            values = chosen(j, h)[:, HS:]
            at_out[j, cols, :] = dot(values, rounded, TN).astype(BF)
            return 0

        lax.fori_loop(0, NZ, att2, 0)
        yg_out[h] = GR[1 - yh, :, wide].astype(BF)
        yg_copy(h).start()

    def at_start(r, _):
        at_copy(lax.rem(z + r, NZ)).start()
        return 0

    lax.fori_loop(1, NZ, at_start, 0)
    at_in[z] = at_out[z]

    def add_mate(h):
        wide = slice(h * 256, h * 256 + 256)
        yg_copy(h).wait_recv()
        kvg[:, wide] = (GR[yh, :, wide] + yg_in[h].astype(F32)).astype(BF)

    for direction in range(2):
        for u in range(4):
            for t in range(4 if u < 2 else 3):
                ag(direction, u, t).wait_send()
    for h in range(2):
        kv_copy(h).wait_send()

    def sent(r, _):
        info_copy(r).wait_send()
        res_copy(r).wait_send()
        far_copy(r).wait_send()
        return 0

    lax.fori_loop(1, NZ, sent, 0)
    for r in near[1:]:
        st_copy(lax.rem(z + r, NZ)).wait_send()
    add_mate(0)

    two, nxt, prv = lax.rem(x + 2, NX), lax.rem(x + 1, NX), lax.rem(x + 3, NX)
    order = [two, nxt, prv, x]

    def w_rows(p, n, core):
        e = (order[n] * 2 + core) * 2 + (1 - m if p == 0 else m)
        return pl.ds(pl.multiple_of(e * 512, 512), 512)

    def half(p, n, core, h):
        wide = slice(h * 256, h * 256 + 256)
        return dot(kvg[:, wide], W[w_rows(p, n, core), wide], NT)

    early = {(0, 0, 0): 0, (0, 1, 0): 1, (0, 2, 0): 2, (0, 0, 1): 3}
    for (p, n, mine), i in early.items():
        PRE[i] = half(p, n, c if mine else 1 - c, 0)
    add_mate(1)

    def product(p, n, mine):
        core = c if mine else 1 - c
        if (p, n, mine) in early:
            return PRE[early[p, n, mine]] + half(p, n, core, 1)
        return dot(kvg[...], W[w_rows(p, n, core), :], NT)

    def cs_copy(p, n):
        return remote(cs_out.at[p, n], cs_in.at[p, n], cs_send.at[p, n], cs_recv.at[p, n], core_mate)

    def for_mate(p, n):
        cs_out[p, n] = product(p, n, 0).astype(BF)
        cs_copy(p, n).start()

    def own(p, n):
        mine = product(p, n, 1)
        cs_copy(p, n).wait_recv()
        R[p, n] = (mine + cs_in[p, n].astype(F32)).astype(BF)

    def by_copy(n):
        return remote(R.at[0, n, ROWS_A:256, :], by_in.at[n], by_send.at[n], by_recv.at[n], m_mate)

    def xsum(src, tmp, into, ssem, rsem):
        def at(n, half):
            return src(n, slice(half * 256, half * 256 + 256))

        firsts = [
            remote(at(0, 0), into.at[0], ssem.at[0], rsem.at[0], x_right),
            remote(at(0, 1), into.at[1], ssem.at[1], rsem.at[1], x_left),
            remote(at(1, 1), into.at[2], ssem.at[2], rsem.at[2], x_right),
            remote(at(2, 0), into.at[3], ssem.at[3], rsem.at[3], x_left),
        ]
        seconds = [
            remote(tmp.at[0], into.at[4], ssem.at[4], rsem.at[4], x_right),
            remote(tmp.at[1], into.at[5], ssem.at[5], rsem.at[5], x_left),
        ]

        def start(n):
            for i in [(0, 1), (2,), (3,), ()][n]:
                firsts[i].start()

        def relay():
            for i in range(2):
                firsts[i].wait_recv()
                tmp[i] = (at(1 + i, i)[...].astype(F32) + into[i].astype(F32)).astype(BF)
                seconds[i].start()

        def finish():
            firsts[2].wait_recv()
            firsts[3].wait_recv()
            seconds[0].wait_recv()
            seconds[1].wait_recv()
            halves = []
            for half, got in [(0, (4, 3)), (1, (2, 5))]:
                v = at(3, half)[...].astype(F32)
                for g in got:
                    v += into[g].astype(F32)
                halves.append(v)
            return halves

        def drain():
            for cp in firsts + seconds:
                cp.wait_send()

        return start, relay, finish, drain

    a0_start, a0_relay, a0_finish, a0_drain = xsum(
        lambda n, cols: R.at[0, n, 0:ROWS_A, cols],
        ax_tmp.at[0], ax_in.at[0], ax_send.at[0], ax_recv.at[0],
    )
    a1_start, a1_relay, a1_finish, a1_drain = xsum(
        lambda n, cols: R.at[1, n, 0:ROWS_A, cols],
        ax_tmp.at[1], ax_in.at[1], ax_send.at[1], ax_recv.at[1],
    )
    b_start, b_relay, b_finish, b_drain = xsum(
        lambda n, cols: RB.at[n, :, cols], bx_tmp, bx_in, bx_send, bx_recv
    )

    def add_b(n):
        by_copy(n).wait_recv()
        RB[n] = (R[1, n, ROWS_A:256, :].astype(F32) + by_in[n].astype(F32)).astype(BF)
        b_start(n)

    ay = remote(ay_out, ay_in, ay_send, ay_recv, m_mate)
    for_mate(0, 0)
    for_mate(0, 1)
    for_mate(0, 2)
    for n in range(NX):
        own(0, n)
        a0_start(n)
        by_copy(n).start()
        for_mate(*((0, 3) if n == 0 else (1, n - 1)))
    a0_relay()
    for n in range(NX):
        own(1, n)
        a1_start(n)
        if n == 0:
            for_mate(1, 3)
    add_b(0)
    fa = a0_finish()
    for half_ in range(2):
        ay_out[:, half_ * 256 : half_ * 256 + 256] = fa[half_].astype(BF)
    ay.start()
    a1_relay()
    add_b(1)
    add_b(2)
    b_relay()
    add_b(3)

    def at_wait(r, _):
        src = lax.rem(z + NZ - r, NZ)
        remote(at_out.at[src], at_in.at[src], at_send.at[r], at_recv.at[r], at_z(src)).wait_recv()
        return 0

    lax.fori_loop(1, NZ, at_wait, 0)
    total = at_in[0].astype(F32)
    for i in range(1, NZ):
        total += at_in[i].astype(F32)
    att_ref[...] = total.T.astype(BF)

    def at_sent(r, _):
        at_copy(lax.rem(z + r, NZ)).wait_send()
        return 0

    lax.fori_loop(1, NZ, at_sent, 0)
    for h in range(2):
        yg_copy(h).wait_send()

    for n in range(NX):
        for p in range(2):
            cs_copy(p, n).wait_send()
        by_copy(n).wait_send()
    fb = b_finish()
    for half in range(2):
        cols = slice(half * 256, half * 256 + 256)
        nbr_ref[ROWS_A:256, cols] = fb[half].astype(BF)
    fa = a1_finish()
    ay.wait_recv()
    for half in range(2):
        cols = slice(half * 256, half * 256 + 256)
        nbr_ref[0:ROWS_A, cols] = (fa[half] + ay_in[:, cols].astype(F32)).astype(BF)

    ay.wait_send()
    a0_drain()
    a1_drain()
    b_drain()


def on_device(nbr_states, kv_weight, queries, out_grad, citations):
    width = kv_weight.shape[0]
    rest = 256 - ROWS_A
    weight = kv_weight.reshape(width, 2, 2, HS).transpose(0, 2, 1, 3).reshape(width * 4, HS)
    V, D = pltpu.VMEM, pltpu.SemaphoreType.DMA
    scratch = [
        V((KC, 256, width // KC), BF),
        V((KC, width * 4 // KC, HS), BF),
        V((width, 512), BF),
        V((256, 256), F32),
        V((NZ, 2, 256, 256), BF),
        V((2, 2, 256, 256), BF),
        V((NZ, 8, 256), F32),
        V((NZ, 8, 256), F32),
        V((NZ, 2, 256, 256), F32),
        V((NZ, 2, 256, 256), F32),
        V((NZ, 8, 256), F32),
        V((NZ, 8, 256), F32),
        V((8, 256), F32),
        V((NZ, 8, 256), F32),
        V((NZ, 8, 256), F32),
        V((NZ, 256, 256), BF),
        V((NZ, 256, 256), BF),
        V((2, 256, 512), F32),
        V((2, 256, 256), BF),
        V((2, 256, 256), BF),
        V((256, 512), BF),
        V((2, NX, 256, 512), BF),
        V((2, NX, 256, 512), BF),
        V((2, NX, 256, 512), BF),
        V((NX, rest, 512), BF),
        V((NX, rest, 512), BF),
        V((2, 6, ROWS_A, 256), BF),
        V((2, 2, ROWS_A, 256), BF),
        V((6, rest, 256), BF),
        V((2, rest, 256), BF),
        V((ROWS_A, 512), BF),
        V((ROWS_A, 512), BF),
        V((256, 256), BF),
        V((4, 256, 512), F32),
        D((2, KC)),
        D((2,)),
        D((2, 4, 4)), D((2, 4, 4)),
        D((2,)), D((2,)),
        D((NZ,)), D((NZ,)),
        D((NZ,)), D((NZ,)),
        D((NZ,)), D((NZ,)),
        D((NZ,)), D((NZ,)),
        D((NZ,)), D((NZ,)),
        D((2,)), D((2,)),
        D((2, NX)), D((2, NX)),
        D((NX,)), D((NX,)),
        D((2, 6)), D((2, 6)),
        D((6,)), D((6,)),
        D, D,
    ]
    vmem = pl.BlockSpec(memory_space=pltpu.VMEM)
    hbm = pl.BlockSpec(memory_space=pl.ANY)
    return pl.pallas_call(
        kernel,
        out_shape=(pltpu.VMEM((256, 256), BF), pltpu.VMEM((256, 512), BF)),
        in_specs=[pl.BlockSpec(memory_space=pltpu.SMEM), hbm, hbm, hbm, hbm],
        out_specs=(vmem, vmem),
        scratch_shapes=scratch,
        compiler_params=pltpu.CompilerParams(
            collective_id=0, has_side_effects=True, vmem_limit_bytes=56 * 2**20
        ),
        cost_estimate=pl.CostEstimate(
            flops=6 * 10**9, bytes_accessed=13 * 2**20, transcendentals=2 * 10**6
        ),
    )(citations.T, queries, out_grad, nbr_states, weight)


def solution(mesh):
    heads = ("section", "mp")
    return jax.shard_map(
        on_device,
        mesh=mesh,
        in_specs=(
            P("dp", None),
            P(None, None, heads),
            P("dp", heads),
            P("dp", heads),
            P("dp", None),
        ),
        out_specs=(P("dp", heads), P("dp", heads)),
        check_vma=False,
    )
```
